32 devices in a mesh: seq: 16 (over z, x, core), head: 2 (over y).
Axes of the slice: x: 2, y: 2, z: 4, core: 2. Of those that a mesh axis runs over, the one named last changes fastest.
Arguments:
- tokens: bfloat16 [2048, 3072], P('seq', 'head'), may hold values from -5 to 5, as said below
- norm_gains: float32 [5, 3072], replicated, may hold values from 0.25 to 1.75
- window: int32 [24], P('head'), may hold values from 16 to 128, as said below
- self_query: bfloat16 [3072, 3072], P(None, 'head')
- self_key_value: bfloat16 [2, 3072, 1024], P(None, None, 'head')
- self_output: bfloat16 [3072, 3072], P('head'), may hold values from -0.4375 to 0.4375
- shared_key_value: bfloat16 [2, 3072, 1024], P(None, None, 'head')
- cross_query: bfloat16 [3, 3072, 3072], P(None, 'seq', 'head')
- cross_output: bfloat16 [3, 3072, 3072], P(None, 'head', 'seq'), may hold values from -0.4375 to 0.4375
- key_blocks: int32 [3, 16, 16], P(None, 'seq'), may hold values from -1 to 15, as said below
Outputs:
- mixed: float32 [2048, 3072], P('seq', 'head')
The draws below stay inside these ranges and needn't reach their ends.
Inputs may be any that keep to these rules, and one draw needn't show every extreme that they name: `tokens`: rows may hold near twins of the rows beside them. Some head has a window of exactly 128 and some head one of exactly 16. `key_blocks`: the row of query block b lists distinct blocks at or before b, the first being b itself; it holds min(16, b + 1) blocks and -1 in the remaining slots.
All inputs are finite; a program needn't handle non-finite values.
Results may differ from the reference program's by a relative error of at most 0.04.
Values may be sent and summed in bfloat16 or wider, within the bound.
No kernel may reach another device: no remote copies, remote signals or barrier semaphores. Data moves between devices by JAX's collectives and lax.ppermute only.
A program may use at most 192 MiB of HBM per device.

```python
import math
import jax
import jax.numpy as jnp
from jax import lax

MODEL_WIDTH = 3072
QUERY_HEADS = 24
KEY_VALUE_HEADS = 8
HEAD_WIDTH = 128
KEY_BLOCK_TOKENS = 128
LISTED_BLOCKS = 16
SECTIONS = 3
TOKENS_PER_INDEX = 128
TOKENS = 2048
SEQUENCE_BLOCKS = 16
N_SEQ = 16
N_HEAD = 2


def draw_tokens(key, part):
    drawn = jnp.clip(jax.random.normal(key, (TOKENS, MODEL_WIDTH), jnp.float32), -4.0, 4.0) * 0.5
    return drawn.astype(jnp.bfloat16)


def key_value_offset(key, selected_index):
    unmasked_sample = jax.random.normal(jax.random.fold_in(key, 11 + selected_index), (2, MODEL_WIDTH, KEY_VALUE_HEADS * HEAD_WIDTH), jnp.float32)
    return jnp.clip(unmasked_sample, -6.0, 6.0) / math.sqrt(MODEL_WIDTH)


def query_base(key, selected_index, count):
    unmasked_sample = jax.random.normal(jax.random.fold_in(key, 21 + selected_index), (count, MODEL_WIDTH, QUERY_HEADS * HEAD_WIDTH), jnp.float32)
    noise = jnp.clip(unmasked_sample, -6.0, 6.0) / math.sqrt(MODEL_WIDTH)
    return noise


def draw_self_query(key, part):
    return query_base(key, 0, 1)[0].astype(jnp.bfloat16)


def draw_self_key_value(key, part):
    return key_value_offset(key, 0).astype(jnp.bfloat16)


def draw_shared_key_value(key, part):
    return key_value_offset(key, 1).astype(jnp.bfloat16)


def draw_cross_query(key, part):
    return query_base(key, 1, SECTIONS).astype(jnp.bfloat16)


def draw_window(key, part):
    widths = jax.random.randint(key, (QUERY_HEADS,), TOKENS_PER_INDEX // 8, TOKENS_PER_INDEX + 1, dtype=jnp.int32)
    widest = jax.random.randint(jax.random.fold_in(key, 5), (), 0, QUERY_HEADS, dtype=jnp.int32)
    step_away = jax.random.randint(jax.random.fold_in(key, 6), (), 1, QUERY_HEADS, dtype=jnp.int32)
    narrow = (widest + step_away) % QUERY_HEADS
    heads = jnp.arange(QUERY_HEADS, dtype=jnp.int32)
    widths = jnp.where(heads == widest, TOKENS_PER_INDEX, widths)
    return jnp.where(heads == narrow, TOKENS_PER_INDEX // 8, widths).astype(jnp.int32)


def draw_key_blocks(key, part):
    blocks = jnp.arange(SEQUENCE_BLOCKS, dtype=jnp.int32)
    noise = jax.random.randint(key, (SECTIONS, SEQUENCE_BLOCKS, SEQUENCE_BLOCKS), 0, 1 << 16, dtype=jnp.int32)
    ranked = noise * SEQUENCE_BLOCKS + blocks[None, None, :]
    earlier = blocks[None, None, :] < blocks[None, :, None]
    ranked = jnp.where(earlier, ranked, -1)
    best, picked = jax.lax.top_k(ranked, LISTED_BLOCKS - 1)
    picked = jnp.where(best >= 0, picked.astype(jnp.int32), -1)
    itself = jnp.broadcast_to(blocks[None, :, None], (SECTIONS, SEQUENCE_BLOCKS, 1))
    return jnp.concatenate([itself, picked], axis=2).astype(jnp.int32)


def block_scale(rng, shape, cuts, least, high):
    level = 1.0
    for axis_at, blocks in cuts:
        steps = jax.random.uniform(jax.random.fold_in(jax.random.fold_in(rng, 6), axis_at), (blocks,), jnp.float32, least / len(cuts), high / len(cuts))
        level = level * jnp.repeat(jnp.exp(steps), shape[axis_at] // blocks).reshape((-1,) + (1,) * (len(shape) - 1 - axis_at))
    return level


def centred(rng, dims, width, bound, split=(), kind=jnp.bfloat16):
    entries = jax.random.normal(rng, dims, jnp.float32) * width
    if len(split) > 0:
        entries = block_scale(rng, dims, split, -0.22, 0.18) * entries
    return jnp.clip(entries, min=-bound, max=bound).astype(kind)


def setup_inputs(seed: int = 0) -> dict:
    key_list = jax.random.split(jax.random.key(seed), 11)
    tokens = draw_tokens(jax.random.fold_in(key_list[10], 71), 0)
    norm_gains = jnp.clip(1.0 + 0.15 * jax.random.normal(key_list[1], (SECTIONS + 2, MODEL_WIDTH), jnp.float32), 0.25, 1.75)
    window = draw_window(jax.random.fold_in(key_list[10], 71), 0)
    self_query = draw_self_query(jax.random.fold_in(key_list[10], 71), 0)
    self_key_value = draw_self_key_value(jax.random.fold_in(key_list[10], 71), 0)
    self_output = centred(key_list[5], (QUERY_HEADS * HEAD_WIDTH, MODEL_WIDTH), (QUERY_HEADS * HEAD_WIDTH // 16) ** -0.5, 0.4375, ((0, 2),))
    shared_key_value = draw_shared_key_value(jax.random.fold_in(key_list[10], 71), 0)
    cross_query = draw_cross_query(jax.random.fold_in(key_list[10], 71), 0)
    cross_output = centred(key_list[8], (SECTIONS, QUERY_HEADS * HEAD_WIDTH, MODEL_WIDTH), (QUERY_HEADS * HEAD_WIDTH // 16) ** -0.5, 0.4375, ((1, 2), (2, 16)))
    key_blocks = draw_key_blocks(jax.random.fold_in(key_list[10], 71), 0)
    return {"tokens": tokens, "norm_gains": norm_gains, "window": window, "self_query": self_query, "self_key_value": self_key_value, "self_output": self_output, "shared_key_value": shared_key_value, "cross_query": cross_query, "cross_output": cross_output, "key_blocks": key_blocks}


EPSILON = 1e-06
MASKED = -1e+30

def normed(stream, gain_row):
    values_f = stream.astype(jnp.float32)
    factor = lax.rsqrt(lax.optimization_barrier(jnp.mean(values_f * values_f, axis=1, keepdims=True)) + EPSILON)
    return (values_f * factor * gain_row[None, :]).astype(jnp.bfloat16)

def project(inputs, weight):
    return jnp.dot(inputs, weight, preferred_element_type=jnp.float32).astype(jnp.bfloat16)

def softmax_rows(scores, allowed):
    scores = jnp.where(allowed, scores, MASKED)
    largest = lax.optimization_barrier(jnp.max(scores, axis=-1, keepdims=True))
    weights = jnp.exp(scores - largest)
    return (weights / lax.optimization_barrier(jnp.sum(weights, axis=-1, keepdims=True))).astype(jnp.bfloat16)

def add_branch(stream, context, out_weight):
    group_cols = context.shape[1] // N_HEAD
    total = stream.astype(jnp.float32)
    for part_index in range(N_HEAD):
        piece = context[:, part_index * group_cols:(part_index + 1) * group_cols]
        weight_rows = out_weight[part_index * group_cols:(part_index + 1) * group_cols]
        term = jnp.dot(piece, weight_rows, preferred_element_type=jnp.float32).astype(jnp.bfloat16)
        term = lax.optimization_barrier(term)
        total = total + term.astype(jnp.float32)
    return total

def window_attention(query_matrix, every_key_row, every_value_row, window):
    query_group_width = QUERY_HEADS // KEY_VALUE_HEADS
    key_rows_extended = jnp.concatenate([jnp.zeros((TOKENS_PER_INDEX, KEY_VALUE_HEADS * HEAD_WIDTH), every_key_row.dtype), every_key_row], axis=0)
    value_rows_extended = jnp.concatenate([jnp.zeros((TOKENS_PER_INDEX, KEY_VALUE_HEADS * HEAD_WIDTH), every_value_row.dtype), every_value_row], axis=0)
    window_bounds = window.reshape(KEY_VALUE_HEADS, query_group_width)
    offsets = jnp.arange(TOKENS_PER_INDEX, dtype=jnp.int32)[:, None] + TOKENS_PER_INDEX - jnp.arange(2 * TOKENS_PER_INDEX, dtype=jnp.int32)[None, :]

    def one_block(block):
        window_begin = (block * TOKENS_PER_INDEX).astype(jnp.int32)
        query_portion = lax.dynamic_slice_in_dim(query_matrix, window_begin, TOKENS_PER_INDEX, 0).reshape(TOKENS_PER_INDEX, KEY_VALUE_HEADS, query_group_width, HEAD_WIDTH).astype(jnp.float32)
        key_portion = lax.dynamic_slice_in_dim(key_rows_extended, window_begin, 2 * TOKENS_PER_INDEX, 0).reshape(2 * TOKENS_PER_INDEX, KEY_VALUE_HEADS, HEAD_WIDTH).astype(jnp.float32)
        value_portion = lax.dynamic_slice_in_dim(value_rows_extended, window_begin, 2 * TOKENS_PER_INDEX, 0).reshape(2 * TOKENS_PER_INDEX, KEY_VALUE_HEADS, HEAD_WIDTH).astype(jnp.float32)
        scores = jnp.einsum('tkgd,skd->kgts', query_portion, key_portion) * HEAD_WIDTH ** (-0.5)
        key_pos = window_begin - TOKENS_PER_INDEX + jnp.arange(2 * TOKENS_PER_INDEX, dtype=jnp.int32)
        allowed = (offsets >= 0)[None, None] & (offsets[None, None] < window_bounds[:, :, None, None]) & (key_pos >= 0)[None, None, None, :]
        probs = softmax_rows(scores, allowed)
        context = jnp.einsum('kgts,skd->tkgd', probs.astype(jnp.float32), value_portion)
        return context.reshape(TOKENS_PER_INDEX, QUERY_HEADS * HEAD_WIDTH).astype(jnp.bfloat16)
    return lax.map(one_block, jnp.arange(N_SEQ, dtype=jnp.int32)).reshape(N_SEQ * TOKENS_PER_INDEX, QUERY_HEADS * HEAD_WIDTH)

def listed_attention(query_matrix, cached_key_rows, cached_value_rows, lists):
    query_group_width = QUERY_HEADS // KEY_VALUE_HEADS
    key_lookup_matrix = cached_key_rows.reshape(SEQUENCE_BLOCKS, KEY_BLOCK_TOKENS, KEY_VALUE_HEADS * HEAD_WIDTH)
    value_lookup_matrix = cached_value_rows.reshape(SEQUENCE_BLOCKS, KEY_BLOCK_TOKENS, KEY_VALUE_HEADS * HEAD_WIDTH)
    inner = jnp.arange(KEY_BLOCK_TOKENS, dtype=jnp.int32)

    def one_block(item):
        block, picks = item
        window_begin = (block * KEY_BLOCK_TOKENS).astype(jnp.int32)
        query_portion = lax.dynamic_slice_in_dim(query_matrix, window_begin, KEY_BLOCK_TOKENS, 0).reshape(KEY_BLOCK_TOKENS, KEY_VALUE_HEADS, query_group_width, HEAD_WIDTH).astype(jnp.float32)
        clamped_index = jnp.maximum(picks, 0).astype(jnp.int32)
        key_portion = jnp.take(key_lookup_matrix, clamped_index, axis=0).reshape(LISTED_BLOCKS * KEY_BLOCK_TOKENS, KEY_VALUE_HEADS, HEAD_WIDTH).astype(jnp.float32)
        value_portion = jnp.take(value_lookup_matrix, clamped_index, axis=0).reshape(LISTED_BLOCKS * KEY_BLOCK_TOKENS, KEY_VALUE_HEADS, HEAD_WIDTH).astype(jnp.float32)
        key_pos = (clamped_index[:, None] * KEY_BLOCK_TOKENS + inner[None, :]).reshape(LISTED_BLOCKS * KEY_BLOCK_TOKENS)
        present = jnp.repeat(picks >= 0, KEY_BLOCK_TOKENS)
        allowed = (present[None, :] & (key_pos[None, :] <= (window_begin + inner)[:, None]))[None, None]
        scores = jnp.einsum('tkgd,skd->kgts', query_portion, key_portion) * HEAD_WIDTH ** (-0.5)
        probs = softmax_rows(scores, allowed)
        context = jnp.einsum('kgts,skd->tkgd', probs.astype(jnp.float32), value_portion)
        return context.reshape(KEY_BLOCK_TOKENS, QUERY_HEADS * HEAD_WIDTH).astype(jnp.bfloat16)
    return lax.map(one_block, (jnp.arange(SEQUENCE_BLOCKS, dtype=jnp.int32), lists)).reshape(SEQUENCE_BLOCKS * KEY_BLOCK_TOKENS, QUERY_HEADS * HEAD_WIDTH)

def reference(tokens, norm_gains, window, self_query, self_key_value, self_output, shared_key_value, cross_query, cross_output, key_blocks):
    first = normed(tokens, norm_gains[0])
    query_matrix = project(first, self_query)
    every_key_row = project(first, self_key_value[0])
    every_value_row = project(first, self_key_value[1])
    context = window_attention(query_matrix, every_key_row, every_value_row, window)
    stream = add_branch(tokens, context, self_output)
    cache_in = normed(stream, norm_gains[1])
    cached_key_rows = project(cache_in, shared_key_value[0])
    cached_value_rows = project(cache_in, shared_key_value[1])
    for section in range(SECTIONS):
        section_in = normed(stream, norm_gains[2 + section])
        query_matrix = project(section_in, cross_query[section])
        context = listed_attention(query_matrix, cached_key_rows, cached_value_rows, key_blocks[section])
        stream = add_branch(stream, context, cross_output[section])
    return stream
```

```python
import functools

import jax
import jax.numpy as jnp
import numpy as np
from jax import lax
from jax.experimental import pallas as pl
from jax.experimental.pallas import tpu as pltpu
from jax.sharding import PartitionSpec as P

HEAD_WIDTH = 128
EPSILON = 1e-06
MASKED = -1e30
CORES = 2


def dot(a, b, contract):
    return lax.dot_general(a, b, ((contract[0], contract[1]), ((), ())), preferred_element_type=jnp.float32)


def listed_kernel(group, lists_ref, q_ref, k_ref, v_ref, o_ref, kg, vg):
    rows = q_ref.shape[0]
    slots = lists_ref.shape[0]
    width = HEAD_WIDTH
    per = 4 if slots % 4 == 0 else 1
    factor = HEAD_WIDTH ** (-0.5) * 1.4426950408889634
    for slot in range(slots):
        at = jnp.maximum(lists_ref[slot], 0) * rows
        at = pl.multiple_of(at, rows)
        kg[slot * rows : (slot + 1) * rows, :] = k_ref[pl.ds(at, rows), :]
        vg[slot * rows : (slot + 1) * rows, :] = v_ref[pl.ds(at, rows), :]
    q = jnp.concatenate([q_ref[:, g * width : (g + 1) * width] for g in range(group)], axis=0)
    own_row = lax.broadcasted_iota(jnp.int32, (rows, rows), 0)
    own_col = lax.broadcasted_iota(jnp.int32, (rows, rows), 1)
    causal = jnp.concatenate([own_col <= own_row] * group, axis=0)
    parts = []
    for start in range(0, slots, per):
        s = dot(q, kg[start * rows : (start + per) * rows, :], ((1,), (1,)))
        pieces = []
        for i in range(per):
            piece = s[:, i * rows : (i + 1) * rows]
            if start + i == 0:
                piece = jnp.where(causal, piece, MASKED)
            else:
                piece = jnp.where(lists_ref[start + i] >= 0, piece, MASKED)
            pieces.append(piece)
        parts.append(jnp.concatenate(pieces, axis=1))
    largest = functools.reduce(jnp.maximum, [jnp.max(p, axis=1, keepdims=True) for p in parts])
    total = jnp.zeros_like(largest)
    acc = jnp.zeros((group * rows, width), jnp.float32)
    for n, p in enumerate(parts):
        weights = jnp.exp2((p - largest) * factor)
        total = total + jnp.sum(weights, axis=1, keepdims=True)
        at = n * per * rows
        acc = acc + dot(weights.astype(jnp.bfloat16), vg[at : at + per * rows, :], ((1,), (0,)))
    acc = acc / total
    for g in range(group):
        o_ref[:, g * width : (g + 1) * width] = acc[g * rows : (g + 1) * rows].astype(o_ref.dtype)


def listed_attention(lists, query, cache, kv_heads):
    rows, columns = query.shape
    keys = cache.shape[0]
    group = columns // (kv_heads * HEAD_WIDTH)
    slots = lists.shape[0]
    spec = pltpu.PrefetchScalarGridSpec(
        num_scalar_prefetch=1,
        grid=(kv_heads,),
        in_specs=[
            pl.BlockSpec((rows, group * HEAD_WIDTH), lambda h, _: (0, h)),
            pl.BlockSpec((keys, HEAD_WIDTH), lambda h, _: (0, h)),
            pl.BlockSpec((keys, HEAD_WIDTH), lambda h, _: (0, kv_heads + h)),
        ],
        out_specs=pl.BlockSpec((rows, group * HEAD_WIDTH), lambda h, _: (0, h)),
        scratch_shapes=[pltpu.VMEM((slots * rows, HEAD_WIDTH), jnp.bfloat16)] * 2,
    )
    return pl.pallas_call(
        functools.partial(listed_kernel, group),
        grid_spec=spec,
        out_shape=jax.ShapeDtypeStruct((rows, columns), jnp.bfloat16),
        compiler_params=pltpu.CompilerParams(vmem_limit_bytes=40 << 20),
        cost_estimate=pl.CostEstimate(
            flops=4 * rows * columns * slots * rows,
            bytes_accessed=2 * cache.size + 4 * query.size,
            transcendentals=rows * slots * rows * columns // HEAD_WIDTH,
        ),
        name="listed_attention",
    )(lists, query, cache, cache)


def query_kernel(count, x_ref, *refs):
    w_refs, o_ref = refs[:count], refs[count]
    piece = x_ref.shape[0] // count
    acc = None
    for j in range(count):
        left = x_ref[j * piece : (j + 1) * piece, :].astype(jnp.float32).T.astype(jnp.bfloat16)
        term = dot(left, w_refs[j][...], ((1,), (0,)))
        acc = term if acc is None else acc + term
    o_ref[...] = acc


def query_project(scaled, pieces):
    columns = pieces[0].shape[1]
    tokens = scaled.shape[1]
    tile = columns // 3
    return pl.pallas_call(
        functools.partial(query_kernel, len(pieces)),
        grid=(columns // tile,),
        in_specs=[pl.BlockSpec(scaled.shape, lambda n: (0, 0))]
        + [pl.BlockSpec((p.shape[0], tile), lambda n: (0, n)) for p in pieces],
        out_specs=pl.BlockSpec((tokens, tile), lambda n: (0, n)),
        out_shape=jax.ShapeDtypeStruct((tokens, columns), jnp.float32),
        compiler_params=pltpu.CompilerParams(vmem_limit_bytes=40 << 20),
        cost_estimate=pl.CostEstimate(
            flops=2 * tokens * columns * scaled.shape[0],
            bytes_accessed=2 * columns * scaled.shape[0] + 4 * tokens * columns,
            transcendentals=0,
        ),
        name="query_project",
    )(scaled, *pieces)


def output_kernel(count, own_ref, other_ref, *refs):
    w_refs, o_ref = refs[:count], refs[count]
    piece = w_refs[0].shape[0]
    context = jnp.concatenate([own_ref[...], other_ref[...]], axis=0)
    for j in range(count):
        term = dot(w_refs[j][...], context, ((1,), (1,)))
        o_ref[j * piece : (j + 1) * piece, :] = term.astype(o_ref.dtype)


def output_project(own, other, pieces):
    features = sum(p.shape[0] for p in pieces)
    tokens = own.shape[0] + other.shape[0]
    return pl.pallas_call(
        functools.partial(output_kernel, len(pieces)),
        out_shape=jax.ShapeDtypeStruct((features, tokens), jnp.bfloat16),
        compiler_params=pltpu.CompilerParams(vmem_limit_bytes=40 << 20),
        cost_estimate=pl.CostEstimate(
            flops=2 * tokens * features * own.shape[1],
            bytes_accessed=2 * features * own.shape[1] + 2 * tokens * features,
            transcendentals=0,
        ),
        name="output_project",
    )(own, other, *pieces)


def body(
    tokens,
    norm_gains,
    window,
    self_query,
    self_key_value,
    self_output,
    shared_key_value,
    cross_query,
    cross_output,
    key_blocks,
):
    seq_count = lax.axis_size("seq")
    head_count = lax.axis_size("head")
    seq_rank = lax.axis_index("seq")
    head_rank = lax.axis_index("head")
    rows = tokens.shape[0]
    model_width = self_query.shape[0]
    kv_columns = self_key_value.shape[2]
    query_columns = self_query.shape[1]
    kv_heads = kv_columns // HEAD_WIDTH
    group = query_columns // kv_columns
    sections = cross_query.shape[0]
    shard = cross_query.shape[1]
    chips = seq_count // CORES
    scale_factor = HEAD_WIDTH ** (-0.5)

    order = list(range(0, chips, 2)) + list(range(1, chips, 2))[::-1]
    place = np.argsort(np.array(order))
    rightward, leftward = [], []
    for core in range(CORES):
        ranks = [chip * CORES + core for chip in order]
        rightward += [(ranks[i], ranks[(i + 1) % chips]) for i in range(chips)]
        leftward += [(ranks[i], ranks[i - 1]) for i in range(chips)]
    twins = [(rank, rank ^ 1) for rank in range(seq_count)]

    my_core = seq_rank % CORES
    my_place = jnp.take(jnp.asarray(place, jnp.int32), seq_rank // CORES)
    ring_chips = jnp.take(jnp.asarray(order, jnp.int32), (my_place + jnp.arange(chips)) % chips)
    own_shards = ring_chips * CORES + my_core
    twin_shards = ring_chips * CORES + (1 - my_core)

    def to_twin(value):
        return lax.ppermute(value, "seq", twins)

    def head_shift(value, k):
        return lax.ppermute(value, "head", [(i, (i + k) % head_count) for i in range(head_count)])

    def over_heads(partial):
        total = partial.astype(jnp.float32)
        for k in range(1, head_count):
            total = total + head_shift(partial, k).astype(jnp.float32)
        return total

    def ring(value, more_right, after):
        pieces = {0: value}
        right = chips // 2 if more_right else chips - 1 - chips // 2
        left = chips - 1 - right
        if after is not None:
            value, _ = lax.optimization_barrier((value, after))
        moving = value
        marks = []
        to_right, to_left = value, value
        for step in range(max(right, left)):
            if step < right:
                to_right = lax.ppermute(to_right, "seq", rightward)
                pieces[-(step + 1) % chips] = to_right
            if step < left:
                to_left = lax.ppermute(to_left, "seq", leftward)
                pieces[step + 1] = to_left
            marks.append((to_right, to_left))
        return [pieces[j] for j in range(chips)], marks

    shards = []
    for s in range(sections):
        shards += [cross_query[s], cross_output[s].T]
    gathered = []
    marks = None
    for m, value in enumerate(shards):
        after = None
        if marks is not None:
            after = marks[0 if m == 1 else 1]
        pieces, marks = ring(value, m % 2 == 0, after)
        gathered.append(pieces)

    parts = [tokens] + [head_shift(tokens, k) for k in range(1, head_count)]
    parts = jnp.stack(parts)
    sources = (head_rank - jnp.arange(head_count)) % head_count
    back = jnp.zeros((head_count,), jnp.int32).at[sources].set(jnp.arange(head_count, dtype=jnp.int32))
    full = jnp.take(parts, back, axis=0).transpose(1, 0, 2).reshape(rows, model_width).astype(jnp.float32)

    def normed(values, gain_row):
        factor = lax.rsqrt(jnp.mean(values * values, axis=1, keepdims=True) + EPSILON)
        return (values * factor * gain_row[None, :]).astype(jnp.bfloat16)

    def project(inputs, weight):
        return jnp.dot(inputs, weight, preferred_element_type=jnp.float32).astype(jnp.bfloat16)

    first = normed(full, norm_gains[0])
    keys_own = project(first, self_key_value[0])
    values_own = project(first, self_key_value[1])
    along = [(i, i + 1) for i in range(seq_count - 1)]
    keys_prev = lax.ppermute(keys_own, "seq", along)
    values_prev = lax.ppermute(values_own, "seq", along)
    query_matrix = project(first, self_query)
    near_keys = jnp.concatenate([keys_prev, keys_own], axis=0).reshape(2 * rows, kv_heads, HEAD_WIDTH)
    near_values = jnp.concatenate([values_prev, values_own], axis=0).reshape(2 * rows, kv_heads, HEAD_WIDTH)
    query_heads = query_matrix.reshape(rows, kv_heads, group, HEAD_WIDTH)
    scores = jnp.einsum("tkgd,skd->kgts", query_heads, near_keys, preferred_element_type=jnp.float32) * scale_factor
    offsets = jnp.arange(rows, dtype=jnp.int32)[:, None] + rows - jnp.arange(2 * rows, dtype=jnp.int32)[None, :]
    key_pos = seq_rank * rows - rows + jnp.arange(2 * rows, dtype=jnp.int32)
    bounds = window.reshape(kv_heads, group)
    allowed = (
        (offsets >= 0)[None, None]
        & (offsets[None, None] < bounds[:, :, None, None])
        & (key_pos >= 0)[None, None, None, :]
    )
    scores = jnp.where(allowed, scores, MASKED)
    weights = jnp.exp(scores - jnp.max(scores, axis=-1, keepdims=True))
    probs = (weights / jnp.sum(weights, axis=-1, keepdims=True)).astype(jnp.bfloat16)
    context = jnp.einsum("kgts,skd->tkgd", probs, near_values, preferred_element_type=jnp.float32)
    context = context.astype(jnp.bfloat16).reshape(rows, query_columns)
    partial = jnp.dot(context, self_output, preferred_element_type=jnp.float32).astype(jnp.bfloat16)
    stream = full + over_heads(partial)

    cache_in = normed(stream, norm_gains[1])
    own_cache = jnp.concatenate(
        [project(cache_in, shared_key_value[0]), project(cache_in, shared_key_value[1])], axis=1
    )
    cache = lax.all_gather(own_cache, "seq", axis=0, tiled=True)

    by_shard = stream.T.reshape(seq_count, shard, rows)
    mine = jnp.take(by_shard, own_shards, axis=0)
    others = to_twin(jnp.take(by_shard, twin_shards, axis=0))
    state = jnp.concatenate([mine, others], axis=2).reshape(chips * shard, CORES * rows)
    gains = jnp.take(norm_gains.reshape(-1, seq_count, shard), own_shards, axis=1).reshape(-1, chips * shard)

    for s in range(sections):
        query_pieces, output_pieces = gathered[2 * s], gathered[2 * s + 1]
        scaled = (state * gains[2 + s][:, None]).astype(jnp.bfloat16)
        squares = jnp.sum(state * state, axis=0)
        partial_query = query_project(scaled, query_pieces)
        from_twin = to_twin(partial_query[rows:].astype(jnp.bfloat16)).astype(jnp.float32)
        squares = squares[:rows] + to_twin(squares[rows:])
        factor = lax.rsqrt(squares / model_width + EPSILON)
        query = ((partial_query[:rows] + from_twin) * factor[:, None]).astype(jnp.bfloat16)
        own = listed_attention(key_blocks[s, 0], query, cache, kv_heads)
        other = to_twin(own)
        partial = output_project(own, other, output_pieces)
        if s < sections - 1:
            state = state + over_heads(partial)

    share = chips // head_count
    per_head = seq_count // head_count

    def of_head(head, value):
        at = jnp.nonzero(own_shards // per_head == head, size=share)[0]
        return jnp.take(value.reshape(chips, shard, CORES * rows), at, axis=0)

    total = of_head(head_rank, partial).astype(jnp.float32)
    for k in range(1, head_count):
        total = total + head_shift(of_head((head_rank + k) % head_count, partial), k).astype(jnp.float32)
    total = of_head(head_rank, state) + total
    kept = total[:, :, :rows]
    brought = to_twin(total[:, :, rows:])
    own_ids = jnp.take(own_shards, jnp.nonzero(own_shards // per_head == head_rank, size=share)[0])
    twin_ids = own_ids + 1 - 2 * my_core
    ids = jnp.concatenate([own_ids, twin_ids]) - head_rank * per_head
    back = jnp.argsort(ids)
    result = jnp.take(jnp.concatenate([kept, brought], axis=0), back, axis=0)
    return result.reshape(per_head * shard, rows).T


def solution(mesh):
    placed = (
        P("seq", "head"),
        P(),
        P("head"),
        P(None, "head"),
        P(None, None, "head"),
        P("head", None),
        P(None, None, "head"),
        P(None, "seq", "head"),
        P(None, "head", "seq"),
        P(None, "seq", None),
    )
    return jax.shard_map(body, mesh=mesh, in_specs=placed, out_specs=P("seq", "head"), check_vma=False)
```

```python
import functools

import jax
import jax.numpy as jnp
import numpy as np
from jax import lax
from jax.experimental import pallas as pl
from jax.experimental.pallas import tpu as pltpu
from jax.sharding import PartitionSpec as P

HEAD_WIDTH = 128
EPSILON = 1e-06
MASKED = -1e30
CORES = 2
SCALE = HEAD_WIDTH ** (-0.5) * 1.4426950408889634
PARAMS = pltpu.CompilerParams(vmem_limit_bytes=44 << 20)
COST = pl.CostEstimate(flops=1, bytes_accessed=1, transcendentals=0)


def dot(a, b, contract):
    return lax.dot_general(a, b, ((contract[0], contract[1]), ((), ())), preferred_element_type=jnp.float32)


def tiles(columns, at_most):
    return next(t for t in range(min(columns, at_most) // 128 * 128, 0, -128) if columns % t == 0)


def normed(values, gain_row):
    factor = lax.rsqrt(jnp.mean(values * values, axis=1, keepdims=True) + EPSILON)
    return (values * factor * gain_row).astype(jnp.bfloat16)


def whole(array):
    rank = len(array.shape)
    return pl.BlockSpec(array.shape, lambda *_: (0,) * rank)


def first_kernel(count, *refs):
    parts, gain_ref, w_ref, x_ref, o_ref = refs[:count], *refs[count:]

    @pl.when((pl.program_id(0) == 0) & (pl.program_id(1) == 0))
    def _():
        values = jnp.concatenate([p[...] for p in parts], axis=1).astype(jnp.float32)
        x_ref[...] = normed(values, gain_ref[...])

    o_ref[...] = dot(x_ref[...], w_ref[0], ((1,), (0,))).astype(o_ref.dtype)


def norm_and_pair(parts, gain, weight):
    rows = parts[0].shape[0]
    _, width, columns = weight.shape
    tile = tiles(columns, 256)
    count = columns // tile
    return pl.pallas_call(
        functools.partial(first_kernel, len(parts)),
        grid=(2, count),
        in_specs=[whole(p) for p in parts]
        + [whole(gain), pl.BlockSpec((1, width, tile), lambda i, n: (i, 0, n))],
        out_specs=[
            pl.BlockSpec((rows, width), lambda i, n: (0, 0)),
            pl.BlockSpec((rows, tile), lambda i, n: (0, i * count + n)),
        ],
        out_shape=[
            jax.ShapeDtypeStruct((rows, width), jnp.bfloat16),
            jax.ShapeDtypeStruct((rows, 2 * columns), jnp.bfloat16),
        ],
        compiler_params=PARAMS,
        cost_estimate=COST,
        name="norm_and_pair",
    )(*parts, gain, weight)


def product_kernel(x_ref, w_ref, o_ref):
    o_ref[...] = dot(x_ref[...], w_ref[...], ((1,), (0,))).astype(o_ref.dtype)


def product(inputs, weight):
    rows, width = inputs.shape
    columns = weight.shape[1]
    tile = tiles(columns, 512 if width > 2048 else 768)
    return pl.pallas_call(
        product_kernel,
        grid=(columns // tile,),
        in_specs=[whole(inputs), pl.BlockSpec((width, tile), lambda n: (0, n))],
        out_specs=pl.BlockSpec((rows, tile), lambda n: (0, n)),
        out_shape=jax.ShapeDtypeStruct((rows, columns), jnp.bfloat16),
        compiler_params=PARAMS,
        cost_estimate=COST,
        name="product",
    )(inputs, weight)


def window_kernel(group, info_ref, q_ref, kp_ref, ko_ref, vp_ref, vo_ref, o_ref):
    rows, width = ko_ref.shape
    head = pl.program_id(0)
    q = jnp.concatenate([q_ref[:, g * width : (g + 1) * width] for g in range(group)], axis=0)
    keys = jnp.concatenate([kp_ref[...], ko_ref[...]], axis=0)
    values = jnp.concatenate([vp_ref[...], vo_ref[...]], axis=0)
    s = dot(q, keys, ((1,), (1,)))
    row = lax.broadcasted_iota(jnp.int32, (rows, 2 * rows), 0)
    col = lax.broadcasted_iota(jnp.int32, (rows, 2 * rows), 1)
    offset = row + rows - col
    seen = (offset >= 0) & ((col >= rows) | (info_ref[0] > 0))
    masks = [seen & (offset < info_ref[1 + head * group + g]) for g in range(group)]
    s = jnp.concatenate(
        [jnp.where(masks[g], s[g * rows : (g + 1) * rows], MASKED) for g in range(group)], axis=0
    )
    weights = jnp.exp2((s - jnp.max(s, axis=1, keepdims=True)) * SCALE)
    total = jnp.sum(weights, axis=1, keepdims=True)
    acc = dot(weights.astype(jnp.bfloat16), values, ((1,), (0,))) / total
    for g in range(group):
        o_ref[:, g * width : (g + 1) * width] = acc[g * rows : (g + 1) * rows].astype(o_ref.dtype)


def window_attention(info, query, before, own, kv_heads):
    rows, columns = query.shape
    group = columns // (kv_heads * HEAD_WIDTH)
    queries = pl.BlockSpec((rows, group * HEAD_WIDTH), lambda h, _: (0, h))
    keys = pl.BlockSpec((rows, HEAD_WIDTH), lambda h, _: (0, h))
    values = pl.BlockSpec((rows, HEAD_WIDTH), lambda h, _: (0, kv_heads + h))
    return pl.pallas_call(
        functools.partial(window_kernel, group),
        grid_spec=pltpu.PrefetchScalarGridSpec(
            num_scalar_prefetch=1,
            grid=(kv_heads,),
            in_specs=[queries, keys, keys, values, values],
            out_specs=queries,
        ),
        out_shape=jax.ShapeDtypeStruct((rows, columns), jnp.bfloat16),
        compiler_params=PARAMS,
        cost_estimate=COST,
        name="window_attention",
    )(info, query, before, own, before, own)


def cache_kernel(count, chips, addends, ids_ref, *refs):
    parts, sums = refs[:count], refs[count : count + addends]
    gain_ref, w_ref, o_ref, mine_ref, others_ref, x_ref, t_ref = refs[count + addends :]
    shard = mine_ref.shape[0] // chips

    @pl.when((pl.program_id(0) == 0) & (pl.program_id(1) == 0))
    def _():
        values = jnp.concatenate([p[...] for p in parts], axis=1).astype(jnp.float32)
        values = values + added([ref[...] for ref in sums])
        x_ref[...] = normed(values, gain_ref[...])
        t_ref[...] = values.T

    o_ref[...] = dot(x_ref[...], w_ref[0], ((1,), (0,))).astype(o_ref.dtype)

    @pl.when((pl.program_id(0) == 1) & (pl.program_id(1) == pl.num_programs(1) - 1))
    def _():
        for j in range(chips):
            for k, ref in enumerate((mine_ref, others_ref)):
                at = pl.multiple_of(ids_ref[k * chips + j] * shard, shard)
                ref[j * shard : (j + 1) * shard, :] = t_ref[pl.ds(at, shard), :]


def cache_and_state(ids, parts, sums, gain, weight, chips):
    rows = parts[0].shape[0]
    _, width, columns = weight.shape
    tile = tiles(columns, 256)
    count = columns // tile
    held = width // CORES
    return pl.pallas_call(
        functools.partial(cache_kernel, len(parts), chips, len(sums)),
        grid_spec=pltpu.PrefetchScalarGridSpec(
            num_scalar_prefetch=1,
            grid=(2, count),
            in_specs=[whole(p) for p in parts]
            + [whole(p) for p in sums]
            + [whole(gain), pl.BlockSpec((1, width, tile), lambda i, n, _: (i, 0, n))],
            out_specs=[
                pl.BlockSpec((rows, tile), lambda i, n, _: (0, i * count + n)),
                pl.BlockSpec((held, rows), lambda i, n, _: (0, 0)),
                pl.BlockSpec((held, rows), lambda i, n, _: (0, 0)),
            ],
            scratch_shapes=[pltpu.VMEM((rows, width), jnp.bfloat16), pltpu.VMEM((width, rows), jnp.float32)],
        ),
        out_shape=[
            jax.ShapeDtypeStruct((rows, 2 * columns), jnp.bfloat16),
            jax.ShapeDtypeStruct((held, rows), jnp.float32),
            jax.ShapeDtypeStruct((held, rows), jnp.float32),
        ],
        compiler_params=PARAMS,
        cost_estimate=COST,
        name="cache_and_state",
    )(ids, *parts, *sums, gain, weight)


def fetch(ids_ref, refs, held, arrived):
    count = arrived.shape[0]
    shard = held.shape[0] // count
    copies = []
    for j in range(count):
        source = refs[j].at[0] if len(refs) > 1 else refs[0].at[ids_ref[j]]
        copies.append(pltpu.make_async_copy(source, held.at[pl.ds(j * shard, shard)], arrived.at[j]))
        copies[-1].start()
    return copies


def added(sums):
    total = sums[0].astype(jnp.float32)
    for value in sums[1:]:
        total = total + value.astype(jnp.float32)
    return total


def query_kernel(states, addends, ids_ref, *refs):
    state_refs, sums = refs[:states], refs[states : states + addends]
    gain_ref, *refs = refs[states + addends :]
    *w_refs, new_ref, own_ref, twin_ref, square_ref, x_ref, held, arrived = refs
    tokens, features = x_ref.shape
    rows = tokens // CORES
    columns = own_ref.shape[1]
    tile = tiles(columns, 512)
    copies = fetch(ids_ref, w_refs, held, arrived)
    squares = jnp.zeros((tokens, 1), jnp.float32)
    part = tiles(features, 512)
    for at in range(0, features, part):
        span = slice(at, at + part)
        value = jnp.concatenate([ref[span, :] for ref in state_refs], axis=1)
        if sums:
            value = value + added([ref[span, :] for ref in sums])
        new_ref[span, :] = value
        turned = value.T
        squares = squares + jnp.sum(turned * turned, axis=1, keepdims=True)
        x_ref[:, span] = (turned * gain_ref[:, span]).astype(jnp.bfloat16)
    square_ref[...] = jnp.broadcast_to(squares, square_ref.shape)
    for copy in copies:
        copy.wait()
    for at in range(0, columns, tile):
        span = slice(at, at + tile)
        acc = dot(x_ref[...], held[:, span], ((1,), (0,)))
        own_ref[:, span] = acc[:rows]
        twin_ref[:, span] = acc[rows:].astype(twin_ref.dtype)


def query_project(ids, states, sums, gain, pieces, count):
    _, shard, columns = pieces[0].shape
    features = states[0].shape[0]
    tokens = sum(s.shape[1] for s in states)
    rows = tokens // CORES
    return pl.pallas_call(
        functools.partial(query_kernel, len(states), len(sums)),
        grid_spec=pltpu.PrefetchScalarGridSpec(
            num_scalar_prefetch=1,
            grid=(1,),
            in_specs=[whole(v) for v in (*states, *sums, gain)] + [pl.BlockSpec(memory_space=pl.ANY)] * len(pieces),
            out_specs=[
                pl.BlockSpec((features, tokens), lambda n, _: (0, 0)),
                pl.BlockSpec((rows, columns), lambda n, _: (0, 0)),
                pl.BlockSpec((rows, columns), lambda n, _: (0, 0)),
                pl.BlockSpec((tokens, 128), lambda n, _: (0, 0)),
            ],
            scratch_shapes=[
                pltpu.VMEM((tokens, features), jnp.bfloat16),
                pltpu.VMEM((features, columns), jnp.bfloat16),
                pltpu.SemaphoreType.DMA((count,)),
            ],
        ),
        out_shape=[
            jax.ShapeDtypeStruct((features, tokens), jnp.float32),
            jax.ShapeDtypeStruct((rows, columns), jnp.float32),
            jax.ShapeDtypeStruct((rows, columns), jnp.bfloat16),
            jax.ShapeDtypeStruct((tokens, 128), jnp.float32),
        ],
        compiler_params=PARAMS,
        cost_estimate=COST,
        name="query_project",
    )(ids, *states, *sums, gain, *pieces)


def listed_kernel(group, width_all, count, seen_ref, qo_ref, qt_ref, so_ref, st_ref, *refs):
    k_refs, v_refs, o_ref = refs[:count], refs[count : 2 * count], refs[2 * count]
    rows = qo_ref.shape[0]
    width = HEAD_WIDTH
    per = 4 if count % 4 == 0 else 1
    factor = lax.rsqrt((so_ref[...] + st_ref[...]) / width_all + EPSILON)
    q = jnp.concatenate(
        [
            (
                (qo_ref[:, g * width : (g + 1) * width] + qt_ref[:, g * width : (g + 1) * width].astype(jnp.float32))
                * factor
            ).astype(jnp.bfloat16)
            for g in range(group)
        ],
        axis=0,
    )
    own_row = lax.broadcasted_iota(jnp.int32, (rows, rows), 0)
    own_col = lax.broadcasted_iota(jnp.int32, (rows, rows), 1)
    causal = jnp.concatenate([own_col <= own_row] * group, axis=0)
    parts = []
    for start in range(0, count, per):
        keys = jnp.concatenate([ref[...] for ref in k_refs[start : start + per]], axis=0)
        s = dot(q, keys, ((1,), (1,)))
        pieces = []
        for i in range(per):
            piece = s[:, i * rows : (i + 1) * rows]
            allowed = causal if start + i == 0 else seen_ref[start + i] > 0
            pieces.append(jnp.where(allowed, piece, MASKED))
        parts.append(jnp.concatenate(pieces, axis=1))
    largest = functools.reduce(jnp.maximum, [jnp.max(p, axis=1, keepdims=True) for p in parts])
    total = jnp.zeros_like(largest)
    acc = jnp.zeros((group * rows, width), jnp.float32)
    for n, p in enumerate(parts):
        weights = jnp.exp2((p - largest) * SCALE)
        total = total + jnp.sum(weights, axis=1, keepdims=True)
        values = jnp.concatenate([ref[...] for ref in v_refs[n * per : (n + 1) * per]], axis=0)
        acc = acc + dot(weights.astype(jnp.bfloat16), values, ((1,), (0,)))
    acc = acc / total
    for g in range(group):
        o_ref[:, g * width : (g + 1) * width] = acc[g * rows : (g + 1) * rows].astype(o_ref.dtype)


def listed_attention(seen, own, brought, squares, twin_squares, blocks, kv_heads, width_all):
    rows, columns = own.shape
    group = columns // (kv_heads * HEAD_WIDTH)
    queries = pl.BlockSpec((rows, group * HEAD_WIDTH), lambda h, _: (0, h))
    sides = pl.BlockSpec((rows, 128), lambda h, _: (0, 0))
    return pl.pallas_call(
        functools.partial(listed_kernel, group, width_all, len(blocks)),
        grid_spec=pltpu.PrefetchScalarGridSpec(
            num_scalar_prefetch=1,
            grid=(kv_heads,),
            in_specs=[queries, queries, sides, sides]
            + [pl.BlockSpec((rows, HEAD_WIDTH), lambda h, _: (0, h)) for _ in blocks]
            + [pl.BlockSpec((rows, HEAD_WIDTH), lambda h, _: (0, kv_heads + h)) for _ in blocks],
            out_specs=queries,
        ),
        out_shape=jax.ShapeDtypeStruct((rows, columns), jnp.bfloat16),
        compiler_params=PARAMS,
        cost_estimate=COST,
        name="listed_attention",
    )(seen, own, brought, squares, twin_squares, *blocks, *blocks)


def output_kernel(ids_ref, own_ref, other_ref, *refs):
    *w_refs, o_ref, held, arrived = refs
    copies = fetch(ids_ref, w_refs, held, arrived)
    context = jnp.concatenate([own_ref[...], other_ref[...]], axis=0)
    shard = held.shape[0] // len(copies)
    for j, copy in enumerate(copies):
        copy.wait()
        at = slice(j * shard, (j + 1) * shard)
        o_ref[at, :] = dot(held[at, :], context, ((1,), (1,))).astype(o_ref.dtype)


def output_project(ids, own, other, pieces, count):
    _, shard, columns = pieces[0].shape
    tokens = own.shape[0] + other.shape[0]
    return pl.pallas_call(
        output_kernel,
        grid_spec=pltpu.PrefetchScalarGridSpec(
            num_scalar_prefetch=1,
            grid=(1,),
            in_specs=[whole(own), whole(other)] + [pl.BlockSpec(memory_space=pl.ANY)] * len(pieces),
            out_specs=pl.BlockSpec((count * shard, tokens), lambda n, _: (0, 0)),
            scratch_shapes=[
                pltpu.VMEM((count * shard, columns), jnp.bfloat16),
                pltpu.SemaphoreType.DMA((count,)),
            ],
        ),
        out_shape=jax.ShapeDtypeStruct((count * shard, tokens), jnp.bfloat16),
        compiler_params=PARAMS,
        cost_estimate=COST,
        name="output_project",
    )(ids, own, other, *pieces)


def last_output_kernel(heads, ids_ref, places_ref, own_ref, other_ref, state_ref, *refs):
    w_refs, refs = refs[: -2 * heads - 2], refs[-2 * heads - 2 :]
    own_refs, twin_refs, held, arrived = refs[:heads], refs[heads : 2 * heads], refs[-2], refs[-1]
    copies = fetch(ids_ref, w_refs, held, arrived)
    context = jnp.concatenate([own_ref[...], other_ref[...]], axis=0)
    rows = own_ref.shape[0]
    shard = held.shape[0] // len(copies)
    share = len(copies) // heads
    for j, copy in enumerate(copies):
        copy.wait()
        at = slice(j * shard, (j + 1) * shard)
        term = dot(held[at, :], context, ((1,), (1,))).astype(jnp.bfloat16)
        place = places_ref[j]
        for k in range(heads):

            @pl.when(place // share == k)
            def _(k=k, term=term, at=at, place=place):
                to = pl.ds(pl.multiple_of((place - k * share) * shard, shard), shard)
                value = state_ref[at, :] + term.astype(jnp.float32) if k == 0 else term
                own_refs[k][to, :] = value[:, :rows]
                twin_refs[k][to, :] = value[:, rows:]


def last_output_project(ids, places, own, other, state, pieces, count, heads):
    _, shard, columns = pieces[0].shape
    rows = own.shape[0]
    held = (count // heads * shard, rows)
    return pl.pallas_call(
        functools.partial(last_output_kernel, heads),
        grid_spec=pltpu.PrefetchScalarGridSpec(
            num_scalar_prefetch=2,
            grid=(1,),
            in_specs=[whole(own), whole(other), whole(state)] + [pl.BlockSpec(memory_space=pl.ANY)] * len(pieces),
            out_specs=[pl.BlockSpec(held, lambda n, *_: (0, 0))] * (2 * heads),
            scratch_shapes=[
                pltpu.VMEM((count * shard, columns), jnp.bfloat16),
                pltpu.SemaphoreType.DMA((count,)),
            ],
        ),
        out_shape=[
            jax.ShapeDtypeStruct(held, jnp.float32 if k == 0 else jnp.bfloat16) for _ in range(2) for k in range(heads)
        ],
        compiler_params=PARAMS,
        cost_estimate=COST,
        name="last_output_project",
    )(ids, places, own, other, state, *pieces)


def result_kernel(heads, shard, at_ref, *refs):
    own, twin, (o_ref, turned) = refs[:heads], refs[heads : 2 * heads], refs[2 * heads :]
    count = own[0].shape[0] // shard
    for k, sums in enumerate((own, twin)):
        for j in range(count):
            span = slice(j * shard, (j + 1) * shard)
            to = pl.ds(pl.multiple_of(at_ref[k * count + j] * shard, shard), shard)
            turned[to, :] = added([ref[span, :] for ref in sums])
    o_ref[...] = turned[...].T


def arrange(at, own, twin, shard):
    features, rows = own[0].shape
    return pl.pallas_call(
        functools.partial(result_kernel, len(own), shard),
        grid_spec=pltpu.PrefetchScalarGridSpec(
            num_scalar_prefetch=1,
            grid=(1,),
            in_specs=[whole(v) for v in (*own, *twin)],
            out_specs=pl.BlockSpec((rows, CORES * features), lambda n, _: (0, 0)),
            scratch_shapes=[pltpu.VMEM((CORES * features, rows), jnp.float32)],
        ),
        out_shape=jax.ShapeDtypeStruct((rows, CORES * features), jnp.float32),
        compiler_params=PARAMS,
        cost_estimate=COST,
        name="arrange",
    )(at, *own, *twin)


def body(
    tokens,
    norm_gains,
    window,
    self_query,
    self_key_value,
    self_output,
    shared_key_value,
    cross_query,
    cross_output,
    key_blocks,
):
    seq_count = lax.axis_size("seq")
    head_count = lax.axis_size("head")
    seq_rank = lax.axis_index("seq")
    head_rank = lax.axis_index("head")
    rows = tokens.shape[0]
    model_width = self_query.shape[0]
    kv_heads = self_key_value.shape[2] // HEAD_WIDTH
    sections, shard = cross_query.shape[:2]
    chips = seq_count // CORES

    order = list(range(0, chips, 2)) + list(range(1, chips, 2))[::-1]
    place = np.argsort(np.array(order))
    rightward, leftward = [], []
    for core in range(CORES):
        ranks = [chip * CORES + core for chip in order]
        rightward += [(ranks[i], ranks[(i + 1) % chips]) for i in range(chips)]
        leftward += [(ranks[i], ranks[i - 1]) for i in range(chips)]
    twins = [(rank, rank ^ 1) for rank in range(seq_count)]

    my_core = seq_rank % CORES
    my_place = jnp.take(jnp.asarray(place, jnp.int32), seq_rank // CORES)
    ring_chips = jnp.take(jnp.asarray(order, jnp.int32), (my_place + jnp.arange(chips)) % chips)
    own_shards = ring_chips * CORES + my_core
    twin_shards = ring_chips * CORES + (1 - my_core)

    def to_twin(value):
        return lax.ppermute(value, "seq", twins)

    def head_shift(value, k):
        return lax.ppermute(value, "head", [(i, (i + k) % head_count) for i in range(head_count)])

    def over_heads(value):
        return [value] + [head_shift(value, k) for k in range(1, head_count)]

    events, hops, found = {}, {}, {}

    def tied(value, name):
        needed = [hop(*at) for at in DONE_BEFORE.get(name, ())]
        if not needed or not jax.tree.leaves(value):
            return value
        return lax.optimization_barrier((value, needed))[0]

    def hop(chain, step):
        if (chain, step) in hops:
            return hops[chain, step]
        more_right = chain % 2 == 0
        right = chips // 2 if more_right else chips - 1 - chips // 2
        left = chips - 1 - right
        if step == 0:
            value = chains[chain]
            found[chain] = {0: value}
            values = [value, value]
        else:
            values = list(hop(chain, step - 1))
        after = START_AFTER.get((chain, step))
        if after is not None:
            after = events[after] if isinstance(after, str) else hop(*after)
            values, _ = lax.optimization_barrier((values, after))
        if step < right:
            values[0] = lax.ppermute(values[0], "seq", rightward)
            found[chain][-(step + 1) % chips] = values[0]
        if step < left:
            values[1] = lax.ppermute(values[1], "seq", leftward)
            found[chain][step + 1] = values[1]
        hops[chain, step] = tuple(values)
        return hops[chain, step]

    def pieces_of(chain):
        for step in range(chips // 2):
            hop(chain, step)
        return [found[chain][j] for j in range(chips)]

    early = lax.all_gather(jnp.stack([cross_query[0], cross_output[0].T]), "seq")
    early = early.reshape(-1, *cross_query.shape[1:])
    chains = {}
    for s in range(1, sections):
        chains[2 * s - 2] = cross_query[s][None]
        chains[2 * s - 1] = cross_output[s].T[None]

    def weights_of(section, which):
        if section == 0:
            return 2 * own_shards + which, [early]
        return jnp.zeros_like(own_shards), pieces_of(2 * section - 2 + which)

    held = over_heads(tokens)
    parts = []
    for j in range(head_count):
        part = held[0]
        for k in range(1, head_count):
            part = jnp.where((head_rank - j) % head_count == k, held[k], part)
        parts.append(part)

    first, own_pair = norm_and_pair(parts, norm_gains[0:1], self_key_value)
    before = lax.ppermute(own_pair, "seq", [(i, i + 1) for i in range(seq_count - 1)])
    query = product(first, self_query)
    info = jnp.concatenate([seq_rank.reshape(1).astype(jnp.int32), window])
    context = window_attention(info, query, before, own_pair, kv_heads)
    sums = over_heads(product(context, self_output))

    ids = jnp.concatenate([own_shards, twin_shards])
    own_cache, mine, others = cache_and_state(ids, parts, sums, norm_gains[1:2], shared_key_value, chips)
    chains[CACHE] = own_cache
    own_blocks = pieces_of(CACHE)
    blocks = own_blocks + [to_twin(block) for block in own_blocks]
    at_blocks = jnp.concatenate([own_shards, twin_shards])
    seen = jnp.any(key_blocks[:, 0, :, None] == at_blocks[None, None, :], axis=1).astype(jnp.int32)
    states, sums = [mine, to_twin(others)], []
    gains = jnp.take(norm_gains.reshape(-1, seq_count, shard), own_shards, axis=1).reshape(-1, chips * shard)

    for s in range(sections):
        sums = tied(sums, f"y{s}")
        states = tied(states, f"q{s}")
        at, query_pieces = weights_of(s, 0)
        state, own, for_twin, squares = query_project(at, states, sums, gains[2 + s][None], query_pieces, chips)
        events[f"q{s}"] = for_twin
        brought = to_twin(for_twin)
        twin_squares = to_twin(squares[rows:])
        brought = tied(brought, f"a{s}")
        own = listed_attention(
            seen[s], own, brought, squares[:rows], twin_squares, blocks, kv_heads, model_width
        )
        events[f"a{s}"] = own
        own = tied(own, f"t{s}")
        other = to_twin(own)
        other = tied(other, f"o{s}")
        at, output_pieces = weights_of(s, 1)
        if s < sections - 1:
            partial = output_project(at, own, other, output_pieces, chips)
            events[f"o{s}"] = partial
            states, sums = [state], over_heads(partial)

    per_head = seq_count // head_count
    share = chips // head_count
    of_head = own_shards // per_head
    ranks = jnp.arange(chips)
    before_it = (of_head[None, :] == of_head[:, None]) & (ranks[None, :] < ranks[:, None])
    slots = jnp.sum(before_it, axis=1, dtype=jnp.int32)
    head_slots = (of_head - head_rank) % head_count * share + slots
    parts = last_output_project(at, head_slots, own, other, state, output_pieces, chips, head_count)
    own_parts, twin_parts = list(parts[:head_count]), parts[head_count:]
    twin_parts = [to_twin(part) for part in twin_parts]
    for k in range(1, head_count):
        own_parts[k] = head_shift(own_parts[k], k)
        twin_parts[k] = head_shift(twin_parts[k], k)
    columns = jnp.sum(
        jnp.where((head_slots[None, :] == jnp.arange(share)[:, None]), own_shards[None, :], 0), axis=1, dtype=jnp.int32
    )
    columns = columns - head_rank * per_head
    other_columns = columns + 1 - 2 * my_core
    return arrange(jnp.concatenate([columns, other_columns]), own_parts, twin_parts, shard)


CACHE = -2
START_AFTER = {(0, 0): (CACHE, 3), (1, 0): (CACHE, 3), (2, 0): (1, 1), (3, 0): (2, 1)}
DONE_BEFORE = {"q0": [(CACHE, 3)]}


def solution(mesh):
    placed = (
        P("seq", "head"),
        P(),
        P("head"),
        P(None, "head"),
        P(None, None, "head"),
        P("head", None),
        P(None, None, "head"),
        P(None, "seq", "head"),
        P(None, "head", "seq"),
        P(None, "seq", None),
    )
    return jax.shard_map(body, mesh=mesh, in_specs=placed, out_specs=P("seq", "head"), check_vma=False)
```

```python
import functools

import jax
import jax.numpy as jnp
import numpy as np
from jax import lax
from jax.experimental import pallas as pl
from jax.experimental.pallas import tpu as pltpu
from jax.sharding import PartitionSpec as P

HEAD_WIDTH = 128
EPSILON = 1e-06
MASKED = -1e30
CORES = 2
SCALE = HEAD_WIDTH ** (-0.5) * 1.4426950408889634
PARAMS = pltpu.CompilerParams(vmem_limit_bytes=44 << 20)
MOST = 44 << 20
COST = pl.CostEstimate(flops=1, bytes_accessed=1, transcendentals=0)


def dot(a, b, contract):
    return lax.dot_general(a, b, ((contract[0], contract[1]), ((), ())), preferred_element_type=jnp.float32)


def tiles(columns, at_most):
    return next(t for t in range(min(columns, at_most) // 128 * 128, 0, -128) if columns % t == 0)


def normed(values, gain_row):
    factor = lax.rsqrt(jnp.mean(values * values, axis=1, keepdims=True) + EPSILON)
    return (values * factor * gain_row).astype(jnp.bfloat16)


def whole(array):
    rank = len(array.shape)
    return pl.BlockSpec(array.shape, lambda *_: (0,) * rank)


def first_kernel(count, *refs):
    parts, gain_ref, w_ref, x_ref, o_ref = refs[:count], *refs[count:]

    @pl.when((pl.program_id(0) == 0) & (pl.program_id(1) == 0))
    def _():
        values = jnp.concatenate([p[...] for p in parts], axis=1).astype(jnp.float32)
        x_ref[...] = normed(values, gain_ref[...])

    o_ref[...] = dot(x_ref[...], w_ref[0], ((1,), (0,))).astype(o_ref.dtype)


def norm_and_pair(parts, gain, weight):
    rows = parts[0].shape[0]
    _, width, columns = weight.shape
    tile = tiles(columns, 256)
    count = columns // tile
    return pl.pallas_call(
        functools.partial(first_kernel, len(parts)),
        grid=(2, count),
        in_specs=[whole(p) for p in parts]
        + [whole(gain), pl.BlockSpec((1, width, tile), lambda i, n: (i, 0, n))],
        out_specs=[
            pl.BlockSpec((rows, width), lambda i, n: (0, 0)),
            pl.BlockSpec((rows, tile), lambda i, n: (0, i * count + n)),
        ],
        out_shape=[
            jax.ShapeDtypeStruct((rows, width), jnp.bfloat16),
            jax.ShapeDtypeStruct((rows, 2 * columns), jnp.bfloat16),
        ],
        compiler_params=PARAMS,
        cost_estimate=COST,
        name="norm_and_pair",
    )(*parts, gain, weight)


def product_kernel(x_ref, w_ref, o_ref):
    o_ref[...] = dot(x_ref[...], w_ref[...], ((1,), (0,))).astype(o_ref.dtype)


def product(inputs, weight):
    rows, width = inputs.shape
    columns = weight.shape[1]
    tile = tiles(columns, 512 if width > 2048 else 768)
    return pl.pallas_call(
        product_kernel,
        grid=(columns // tile,),
        in_specs=[whole(inputs), pl.BlockSpec((width, tile), lambda n: (0, n))],
        out_specs=pl.BlockSpec((rows, tile), lambda n: (0, n)),
        out_shape=jax.ShapeDtypeStruct((rows, columns), jnp.bfloat16),
        compiler_params=PARAMS,
        cost_estimate=COST,
        name="product",
    )(inputs, weight)


def window_kernel(group, info_ref, q_ref, kp_ref, ko_ref, vp_ref, vo_ref, o_ref):
    rows, width = ko_ref.shape
    head = pl.program_id(0)
    q = jnp.concatenate([q_ref[:, g * width : (g + 1) * width] for g in range(group)], axis=0)
    keys = jnp.concatenate([kp_ref[...], ko_ref[...]], axis=0)
    values = jnp.concatenate([vp_ref[...], vo_ref[...]], axis=0)
    s = dot(q, keys, ((1,), (1,)))
    row = lax.broadcasted_iota(jnp.int32, (rows, 2 * rows), 0)
    col = lax.broadcasted_iota(jnp.int32, (rows, 2 * rows), 1)
    offset = row + rows - col
    seen = (offset >= 0) & ((col >= rows) | (info_ref[0] > 0))
    masks = [seen & (offset < info_ref[1 + head * group + g]) for g in range(group)]
    s = jnp.concatenate(
        [jnp.where(masks[g], s[g * rows : (g + 1) * rows], MASKED) for g in range(group)], axis=0
    )
    weights = jnp.exp2((s - jnp.max(s, axis=1, keepdims=True)) * SCALE)
    total = jnp.sum(weights, axis=1, keepdims=True)
    acc = dot(weights.astype(jnp.bfloat16), values, ((1,), (0,))) / total
    for g in range(group):
        o_ref[:, g * width : (g + 1) * width] = acc[g * rows : (g + 1) * rows].astype(o_ref.dtype)


def window_attention(info, query, before, own, kv_heads):
    rows, columns = query.shape
    group = columns // (kv_heads * HEAD_WIDTH)
    queries = pl.BlockSpec((rows, group * HEAD_WIDTH), lambda h, _: (0, h))
    keys = pl.BlockSpec((rows, HEAD_WIDTH), lambda h, _: (0, h))
    values = pl.BlockSpec((rows, HEAD_WIDTH), lambda h, _: (0, kv_heads + h))
    return pl.pallas_call(
        functools.partial(window_kernel, group),
        grid_spec=pltpu.PrefetchScalarGridSpec(
            num_scalar_prefetch=1,
            grid=(kv_heads,),
            in_specs=[queries, keys, keys, values, values],
            out_specs=queries,
        ),
        out_shape=jax.ShapeDtypeStruct((rows, columns), jnp.bfloat16),
        compiler_params=PARAMS,
        cost_estimate=COST,
        name="window_attention",
    )(info, query, before, own, before, own)


def cache_kernel(count, chips, addends, ids_ref, *refs):
    parts, sums = refs[:count], refs[count : count + addends]
    gain_ref, w_ref, o_ref, mine_ref, others_ref, x_ref, t_ref = refs[count + addends :]
    shard = mine_ref.shape[0] // chips

    @pl.when((pl.program_id(0) == 0) & (pl.program_id(1) == 0))
    def _():
        values = jnp.concatenate([p[...] for p in parts], axis=1).astype(jnp.float32)
        values = values + added([ref[...] for ref in sums])
        x_ref[...] = normed(values, gain_ref[...])
        t_ref[...] = values.T

    o_ref[...] = dot(x_ref[...], w_ref[0], ((1,), (0,))).astype(o_ref.dtype)

    @pl.when((pl.program_id(0) == 1) & (pl.program_id(1) == pl.num_programs(1) - 1))
    def _():
        for j in range(chips):
            for k, ref in enumerate((mine_ref, others_ref)):
                at = pl.multiple_of(ids_ref[k * chips + j] * shard, shard)
                ref[j * shard : (j + 1) * shard, :] = t_ref[pl.ds(at, shard), :]


def cache_and_state(ids, parts, sums, gain, weight, chips):
    rows = parts[0].shape[0]
    _, width, columns = weight.shape
    tile = tiles(columns, 256)
    count = columns // tile
    held = width // CORES
    return pl.pallas_call(
        functools.partial(cache_kernel, len(parts), chips, len(sums)),
        grid_spec=pltpu.PrefetchScalarGridSpec(
            num_scalar_prefetch=1,
            grid=(2, count),
            in_specs=[whole(p) for p in parts]
            + [whole(p) for p in sums]
            + [whole(gain), pl.BlockSpec((1, width, tile), lambda i, n, _: (i, 0, n))],
            out_specs=[
                pl.BlockSpec((rows, tile), lambda i, n, _: (0, i * count + n)),
                pl.BlockSpec((held, rows), lambda i, n, _: (0, 0)),
                pl.BlockSpec((held, rows), lambda i, n, _: (0, 0)),
            ],
            scratch_shapes=[pltpu.VMEM((rows, width), jnp.bfloat16), pltpu.VMEM((width, rows), jnp.float32)],
        ),
        out_shape=[
            jax.ShapeDtypeStruct((rows, 2 * columns), jnp.bfloat16),
            jax.ShapeDtypeStruct((held, rows), jnp.float32),
            jax.ShapeDtypeStruct((held, rows), jnp.float32),
        ],
        compiler_params=PARAMS,
        cost_estimate=COST,
        name="cache_and_state",
    )(ids, *parts, *sums, gain, weight)


def fetch(refs, held, arrived):
    count = arrived.shape[0]
    shard = held.shape[0] // count
    copies = []
    for j in range(count):
        copies.append(pltpu.make_async_copy(refs[j].at[0], held.at[pl.ds(j * shard, shard)], arrived.at[j]))
        copies[-1].start()
    return copies


def added(sums):
    total = sums[0].astype(jnp.float32)
    for value in sums[1:]:
        total = total + value.astype(jnp.float32)
    return total


def query_kernel(states, addends, *refs):
    state_refs, sums = refs[:states], refs[states : states + addends]
    gain_ref, *refs = refs[states + addends :]
    *w_refs, new_ref, own_ref, twin_ref, square_ref, x_ref, held, arrived = refs
    tokens, features = x_ref.shape
    rows = tokens // CORES
    columns = own_ref.shape[1]
    tile = tiles(columns, 512)
    copies = fetch(w_refs, held, arrived)
    squares = jnp.zeros((tokens, 1), jnp.float32)
    part = tiles(features, 512)
    for at in range(0, features, part):
        span = slice(at, at + part)
        value = jnp.concatenate([ref[span, :] for ref in state_refs], axis=1)
        if sums:
            value = value + added([ref[span, :] for ref in sums])
        new_ref[span, :] = value
        turned = value.T
        squares = squares + jnp.sum(turned * turned, axis=1, keepdims=True)
        x_ref[:, span] = (turned * gain_ref[:, span]).astype(jnp.bfloat16)
    square_ref[...] = jnp.broadcast_to(squares, square_ref.shape)
    for copy in copies:
        copy.wait()
    for at in range(0, columns, tile):
        span = slice(at, at + tile)
        acc = dot(x_ref[...], held[:, span], ((1,), (0,)))
        own_ref[:, span] = acc[:rows]
        twin_ref[:, span] = acc[rows:].astype(twin_ref.dtype)


def query_project(states, sums, gain, pieces):
    _, shard, columns = pieces[0].shape
    count = len(pieces)
    features = states[0].shape[0]
    tokens = sum(s.shape[1] for s in states)
    rows = tokens // CORES
    return pl.pallas_call(
        functools.partial(query_kernel, len(states), len(sums)),
        grid_spec=pltpu.PrefetchScalarGridSpec(
            num_scalar_prefetch=0,
            grid=(1,),
            in_specs=[whole(v) for v in (*states, *sums, gain)] + [pl.BlockSpec(memory_space=pl.ANY)] * len(pieces),
            out_specs=[
                pl.BlockSpec((features, tokens), lambda n: (0, 0)),
                pl.BlockSpec((rows, columns), lambda n: (0, 0)),
                pl.BlockSpec((rows, columns), lambda n: (0, 0)),
                pl.BlockSpec((tokens, 128), lambda n: (0, 0)),
            ],
            scratch_shapes=[
                pltpu.VMEM((tokens, features), jnp.bfloat16),
                pltpu.VMEM((features, columns), jnp.bfloat16),
                pltpu.SemaphoreType.DMA((count,)),
            ],
        ),
        out_shape=[
            jax.ShapeDtypeStruct((features, tokens), jnp.float32),
            jax.ShapeDtypeStruct((rows, columns), jnp.float32),
            jax.ShapeDtypeStruct((rows, columns), jnp.bfloat16),
            jax.ShapeDtypeStruct((tokens, 128), jnp.float32),
        ],
        compiler_params=pltpu.CompilerParams(vmem_limit_bytes=MOST),
        cost_estimate=COST,
        name="query_project",
    )(*states, *sums, gain, *pieces)


def listed_kernel(group, held, width_all, count, seen_ref, qo_ref, qt_ref, so_ref, st_ref, *refs):
    k_refs, v_refs, o_ref = refs[:count], refs[count : 2 * count], refs[2 * count]
    rows = qo_ref.shape[0]
    width = HEAD_WIDTH
    per = 4 if count % 4 == 0 else 1
    factor = lax.rsqrt((so_ref[...] + st_ref[...]) / width_all + EPSILON)
    own_row = lax.broadcasted_iota(jnp.int32, (rows, rows), 0)
    own_col = lax.broadcasted_iota(jnp.int32, (rows, rows), 1)
    causal = jnp.concatenate([own_col <= own_row] * group, axis=0)
    for head in range(held):
        lanes = slice(head * width, (head + 1) * width)
        heads = [slice((head * group + g) * width, (head * group + g + 1) * width) for g in range(group)]
        q = jnp.concatenate(
            [((qo_ref[:, at] + qt_ref[:, at].astype(jnp.float32)) * factor).astype(jnp.bfloat16) for at in heads],
            axis=0,
        )
        parts = []
        for start in range(0, count, per):
            keys = jnp.concatenate([ref[:, lanes] for ref in k_refs[start : start + per]], axis=0)
            s = dot(q, keys, ((1,), (1,)))
            pieces = []
            for i in range(per):
                piece = s[:, i * rows : (i + 1) * rows]
                allowed = causal if start + i == 0 else seen_ref[start + i] > 0
                pieces.append(jnp.where(allowed, piece, MASKED))
            parts.append(jnp.concatenate(pieces, axis=1))
        largest = functools.reduce(jnp.maximum, [jnp.max(p, axis=1, keepdims=True) for p in parts])
        total = jnp.zeros_like(largest)
        acc = jnp.zeros((group * rows, width), jnp.float32)
        for n, p in enumerate(parts):
            weights = jnp.exp2((p - largest) * SCALE)
            total = total + jnp.sum(weights, axis=1, keepdims=True)
            values = jnp.concatenate([ref[:, lanes] for ref in v_refs[n * per : (n + 1) * per]], axis=0)
            acc = acc + dot(weights.astype(jnp.bfloat16), values, ((1,), (0,)))
        acc = acc / total
        for g, at in enumerate(heads):
            o_ref[:, at] = acc[g * rows : (g + 1) * rows].astype(o_ref.dtype)


def listed_attention(seen, own, brought, squares, twin_squares, blocks, kv_heads, width_all):
    rows, columns = own.shape
    group = columns // (kv_heads * HEAD_WIDTH)
    held = HEADS_AT_ONCE if kv_heads % HEADS_AT_ONCE == 0 else 1
    steps = kv_heads // held
    queries = pl.BlockSpec((rows, held * group * HEAD_WIDTH), lambda h, _: (0, h))
    sides = pl.BlockSpec((rows, 128), lambda h, _: (0, 0))
    return pl.pallas_call(
        functools.partial(listed_kernel, group, held, width_all, len(blocks)),
        grid_spec=pltpu.PrefetchScalarGridSpec(
            num_scalar_prefetch=1,
            grid=(steps,),
            in_specs=[queries, queries, sides, sides]
            + [pl.BlockSpec((rows, held * HEAD_WIDTH), lambda h, _: (0, h)) for _ in blocks]
            + [pl.BlockSpec((rows, held * HEAD_WIDTH), lambda h, _: (0, steps + h)) for _ in blocks],
            out_specs=queries,
        ),
        out_shape=jax.ShapeDtypeStruct((rows, columns), jnp.bfloat16),
        compiler_params=PARAMS,
        cost_estimate=COST,
        name="listed_attention",
    )(seen, own, brought, squares, twin_squares, *blocks, *blocks)


def output_kernel(own_ref, other_ref, *refs):
    *w_refs, o_ref, held, arrived = refs
    copies = fetch(w_refs, held, arrived)
    context = jnp.concatenate([own_ref[...], other_ref[...]], axis=0)
    shard = held.shape[0] // len(copies)
    for j in range(0, len(copies), AT_ONCE):
        for copy in copies[j : j + AT_ONCE]:
            copy.wait()
        at = slice(j * shard, min(j + AT_ONCE, len(copies)) * shard)
        o_ref[at, :] = dot(held[at, :], context, ((1,), (1,))).astype(o_ref.dtype)


def output_project(own, other, pieces):
    _, shard, columns = pieces[0].shape
    count = len(pieces)
    tokens = own.shape[0] + other.shape[0]
    return pl.pallas_call(
        output_kernel,
        grid_spec=pltpu.PrefetchScalarGridSpec(
            num_scalar_prefetch=0,
            grid=(1,),
            in_specs=[whole(own), whole(other)] + [pl.BlockSpec(memory_space=pl.ANY)] * len(pieces),
            out_specs=pl.BlockSpec((count * shard, tokens), lambda n: (0, 0)),
            scratch_shapes=[
                pltpu.VMEM((count * shard, columns), jnp.bfloat16),
                pltpu.SemaphoreType.DMA((count,)),
            ],
        ),
        out_shape=jax.ShapeDtypeStruct((count * shard, tokens), jnp.bfloat16),
        compiler_params=pltpu.CompilerParams(vmem_limit_bytes=MOST),
        cost_estimate=COST,
        name="output_project",
    )(own, other, *pieces)


def last_output_kernel(heads, share, places_ref, own_ref, other_ref, state_ref, *refs):
    w_refs, refs = refs[: -2 * heads - 2], refs[-2 * heads - 2 :]
    own_refs, twin_refs, held, arrived = refs[:heads], refs[heads : 2 * heads], refs[-2], refs[-1]
    copies = fetch(w_refs, held, arrived)
    context = jnp.concatenate([own_ref[...], other_ref[...]], axis=0)
    rows = own_ref.shape[0]
    shard = held.shape[0] // len(copies)
    if len(copies) > 1:
        for ref in (*own_refs, *twin_refs):
            ref[...] = jnp.zeros_like(ref)
    for copy in copies:
        copy.wait()
    terms = dot(held[...], context, ((1,), (1,))).astype(jnp.bfloat16)
    for j in range(len(copies)):
        at = slice(j * shard, (j + 1) * shard)
        for k in range(heads):
            value = state_ref[at, :] + terms[at].astype(jnp.float32) if k == 0 else terms[at]
            if len(copies) == 1:
                own_refs[k][...] = value[:, :rows]
                twin_refs[k][...] = value[:, rows:]
                continue
            place = places_ref[j]

            @pl.when(place // share == k)
            def _(k=k, value=value, place=place):
                to = pl.ds(pl.multiple_of((place - k * share) * shard, shard), shard)
                own_refs[k][to, :] = value[:, :rows]
                twin_refs[k][to, :] = value[:, rows:]


def last_output_project(places, own, other, state, pieces, heads, share):
    _, shard, columns = pieces[0].shape
    count = len(pieces)
    rows = own.shape[0]
    held = ((share if count > 1 else 1) * shard, rows)
    return pl.pallas_call(
        functools.partial(last_output_kernel, heads, share),
        grid_spec=pltpu.PrefetchScalarGridSpec(
            num_scalar_prefetch=1,
            grid=(1,),
            in_specs=[whole(own), whole(other), whole(state)] + [pl.BlockSpec(memory_space=pl.ANY)] * count,
            out_specs=[pl.BlockSpec(held, lambda n, *_: (0, 0))] * (2 * heads),
            scratch_shapes=[
                pltpu.VMEM((count * shard, columns), jnp.bfloat16),
                pltpu.SemaphoreType.DMA((count,)),
            ],
        ),
        out_shape=[
            jax.ShapeDtypeStruct(held, jnp.float32 if k == 0 else jnp.bfloat16) for _ in range(2) for k in range(heads)
        ],
        compiler_params=pltpu.CompilerParams(vmem_limit_bytes=MOST),
        cost_estimate=COST,
        name="last_output_project",
    )(places, own, other, state, *pieces)


def result_kernel(heads, shard, at_ref, *refs):
    own, twin, own_late, twin_late = (refs[k * heads : (k + 1) * heads] for k in range(4))
    o_ref, turned = refs[4 * heads :]
    count = own[0].shape[0] // shard
    for k, (sums, late) in enumerate(((own, own_late), (twin, twin_late))):
        for j in range(count):
            span = slice(j * shard, (j + 1) * shard)
            to = pl.ds(pl.multiple_of(at_ref[k * (count + 1) + j] * shard, shard), shard)
            turned[to, :] = added([ref[span, :] for ref in sums])
        place = at_ref[k * (count + 1) + count]

        @pl.when(place >= 0)
        def _(late=late, place=place):
            to = pl.ds(pl.multiple_of(jnp.maximum(place, 0) * shard, shard), shard)
            turned[to, :] = added([ref[...] for ref in late])

    o_ref[...] = turned[...].T


def arrange(at, parts, shard):
    features, rows = parts[0][0].shape
    return pl.pallas_call(
        functools.partial(result_kernel, len(parts[0]), shard),
        grid_spec=pltpu.PrefetchScalarGridSpec(
            num_scalar_prefetch=1,
            grid=(1,),
            in_specs=[whole(v) for part in parts for v in part],
            out_specs=pl.BlockSpec((rows, CORES * features), lambda n, _: (0, 0)),
            scratch_shapes=[pltpu.VMEM((CORES * features, rows), jnp.float32)],
        ),
        out_shape=jax.ShapeDtypeStruct((rows, CORES * features), jnp.float32),
        compiler_params=PARAMS,
        cost_estimate=COST,
        name="arrange",
    )(at, *[v for part in parts for v in part])


def body(
    tokens,
    norm_gains,
    window,
    self_query,
    self_key_value,
    self_output,
    shared_key_value,
    cross_query,
    cross_output,
    key_blocks,
):
    seq_count = lax.axis_size("seq")
    head_count = lax.axis_size("head")
    seq_rank = lax.axis_index("seq")
    head_rank = lax.axis_index("head")
    rows = tokens.shape[0]
    model_width = self_query.shape[0]
    kv_heads = self_key_value.shape[2] // HEAD_WIDTH
    sections, shard = cross_query.shape[:2]
    chips = seq_count // CORES

    order = list(range(0, chips, 2)) + list(range(1, chips, 2))[::-1]
    place = np.argsort(np.array(order))
    rightward, leftward = [], []
    for core in range(CORES):
        ranks = [chip * CORES + core for chip in order]
        rightward += [(ranks[i], ranks[(i + 1) % chips]) for i in range(chips)]
        leftward += [(ranks[i], ranks[i - 1]) for i in range(chips)]
    twins = [(rank, rank ^ 1) for rank in range(seq_count)]

    my_core = seq_rank % CORES
    my_place = jnp.take(jnp.asarray(place, jnp.int32), seq_rank // CORES)
    ring_chips = jnp.take(jnp.asarray(order, jnp.int32), (my_place + jnp.arange(chips)) % chips)
    own_shards = ring_chips * CORES + my_core
    twin_shards = ring_chips * CORES + (1 - my_core)

    def to_twin(value):
        return lax.ppermute(value, "seq", twins)

    def head_shift(value, k):
        return lax.ppermute(value, "head", [(i, (i + k) % head_count) for i in range(head_count)])

    def over_heads(value):
        return [value] + [head_shift(value, k) for k in range(1, head_count)]

    events, hops, found = {}, {}, {}

    def tied(value, name):
        needed = [hop(*at) for at in DONE_BEFORE.get(name, ())]
        if not needed or not jax.tree.leaves(value):
            return value
        return lax.optimization_barrier((value, needed))[0]

    def hop(chain, step):
        if (chain, step) in hops:
            return hops[chain, step]
        more_right = chain % 2 == 0
        right = chips // 2 if more_right else chips - 1 - chips // 2
        left = chips - 1 - right
        if step == 0:
            value = chains[chain]
            found[chain] = {0: value}
            values = [value, value]
        else:
            values = list(hop(chain, step - 1))
        after = START_AFTER.get((chain, step))
        if after is not None:
            after = events[after] if isinstance(after, str) else hop(*after)
            values, _ = lax.optimization_barrier((values, after))
        if step < right:
            values[0] = lax.ppermute(values[0], "seq", rightward)
            found[chain][-(step + 1) % chips] = values[0]
        if step < left:
            values[1] = lax.ppermute(values[1], "seq", leftward)
            found[chain][step + 1] = values[1]
        hops[chain, step] = tuple(values)
        return hops[chain, step]

    def pieces_of(chain):
        for step in range(chips // 2):
            hop(chain, step)
        return [found[chain][j] for j in range(chips)]

    chains = {}
    for s in range(sections):
        chains[2 * s] = cross_query[s][None]
        chains[2 * s + 1] = cross_output[s].T[None]

    held = over_heads(tokens)
    parts = []
    for j in range(head_count):
        part = held[0]
        for k in range(1, head_count):
            part = jnp.where((head_rank - j) % head_count == k, held[k], part)
        parts.append(part)

    parts = tied(parts, "f0")
    first, own_pair = norm_and_pair(parts, norm_gains[0:1], self_key_value)
    before = lax.ppermute(own_pair, "seq", [(i, i + 1) for i in range(seq_count - 1)])
    query = product(first, self_query)
    info = jnp.concatenate([seq_rank.reshape(1).astype(jnp.int32), window])
    query = tied(query, "f1")
    context = window_attention(info, query, before, own_pair, kv_heads)
    sums = over_heads(product(context, self_output))

    sums = tied(sums, "f2")
    ids = jnp.concatenate([own_shards, twin_shards])
    own_cache, mine, others = cache_and_state(ids, parts, sums, norm_gains[1:2], shared_key_value, chips)
    chains[CACHE] = own_cache
    events["cache"] = own_cache
    own_blocks = pieces_of(CACHE)
    blocks = own_blocks + [to_twin(block) for block in own_blocks]
    at_blocks = jnp.concatenate([own_shards, twin_shards])
    seen = jnp.any(key_blocks[:, 0, :, None] == at_blocks[None, None, :], axis=1).astype(jnp.int32)
    states, sums = [mine, to_twin(others)], []
    gains = jnp.take(norm_gains.reshape(-1, seq_count, shard), own_shards, axis=1).reshape(-1, chips * shard)

    for s in range(sections):
        sums = tied(sums, f"y{s}")
        states = tied(states, f"q{s}")
        query_pieces = pieces_of(2 * s)
        state, own, for_twin, squares = query_project(states, sums, gains[2 + s][None], query_pieces)
        events[f"q{s}"] = for_twin
        brought = to_twin(for_twin)
        twin_squares = to_twin(squares[rows:])
        brought = tied(brought, f"a{s}")
        own = listed_attention(
            seen[s], own, brought, squares[:rows], twin_squares, blocks, kv_heads, model_width
        )
        events[f"a{s}"] = own
        own = tied(own, f"t{s}")
        other = to_twin(own)
        other = tied(other, f"o{s}")
        output_pieces = pieces_of(2 * s + 1)
        if s < sections - 1:
            partial = output_project(own, other, output_pieces)
            events[f"o{s}"] = partial
            states, sums = [state], over_heads(partial)

    per_head = seq_count // head_count
    share = chips // head_count
    of_head = own_shards // per_head
    ranks = jnp.arange(chips)
    before_it = (of_head[None, :] == of_head[:, None]) & (ranks[None, :] < ranks[:, None])
    slots = jnp.sum(before_it, axis=1, dtype=jnp.int32)
    head_slots = (of_head - head_rank) % head_count * share + slots
    late = chips // 2
    early_ones = [j for j in range(chips) if j != late]
    state_pieces = state.reshape(chips, shard, CORES * rows)
    early_state = jnp.concatenate([state_pieces[:late], state_pieces[late + 1 :]]).reshape(-1, CORES * rows)

    def exchanged(parts):
        own_parts, twin_parts = list(parts[:head_count]), [to_twin(part) for part in parts[head_count:]]
        for k in range(1, head_count):
            own_parts[k] = head_shift(own_parts[k], k)
            twin_parts[k] = head_shift(twin_parts[k], k)
        return [own_parts, twin_parts]

    early_parts = last_output_project(
        jnp.take(head_slots, jnp.asarray(early_ones)),
        own,
        other,
        early_state,
        [output_pieces[j] for j in early_ones],
        head_count,
        share,
    )
    early_parts = exchanged(early_parts)
    late_parts = exchanged(
        last_output_project(
            head_slots[late : late + 1], own, other, state_pieces[late], [output_pieces[late]], head_count, share
        )
    )
    columns = jnp.sum(
        jnp.where((head_slots[None, :] == jnp.arange(share)[:, None]), own_shards[None, :], 0), axis=1, dtype=jnp.int32
    )
    columns = columns - head_rank * per_head
    late_column = jnp.where(head_slots[late] < share, own_shards[late] - head_rank * per_head, -1)
    flip = 1 - 2 * my_core
    places = [columns, late_column[None], columns + flip, jnp.where(late_column >= 0, late_column + flip, -1)[None]]
    return arrange(jnp.concatenate(places).astype(jnp.int32), early_parts + late_parts, shard)


CACHE = -2
START_AFTER = {(1, 0): (0, 0), (2, 0): (1, 1), (3, 0): (2, 1), (4, 0): (3, 1), (5, 0): (4, 1)}
DONE_BEFORE = {"f0": [(0, 0)], "f1": [(0, 1)], "f2": [(1, 0), (0, 2)]}
HEADS_AT_ONCE = 4
AT_ONCE = 8


def solution(mesh):
    placed = (
        P("seq", "head"),
        P(),
        P("head"),
        P(None, "head"),
        P(None, None, "head"),
        P("head", None),
        P(None, None, "head"),
        P(None, "seq", "head"),
        P(None, "head", "seq"),
        P(None, "seq", None),
    )
    return jax.shard_map(body, mesh=mesh, in_specs=placed, out_specs=P("seq", "head"), check_vma=False)
```

```python
import functools

import jax
import jax.numpy as jnp
import numpy as np
from jax import lax
from jax.experimental import pallas as pl
from jax.experimental.pallas import tpu as pltpu
from jax.sharding import PartitionSpec as P

HEAD_WIDTH = 128
EPSILON = 1e-06
MASKED = -1e30
CORES = 2
SCALE = HEAD_WIDTH ** (-0.5) * 1.4426950408889634
PARAMS = pltpu.CompilerParams(vmem_limit_bytes=44 << 20)
MOST = 44 << 20
COST = pl.CostEstimate(flops=1, bytes_accessed=1, transcendentals=0)


def dot(a, b, contract):
    return lax.dot_general(a, b, ((contract[0], contract[1]), ((), ())), preferred_element_type=jnp.float32)


def tiles(columns, at_most):
    return next(t for t in range(min(columns, at_most) // 128 * 128, 0, -128) if columns % t == 0)


def normed(values, gain_row):
    factor = lax.rsqrt(jnp.mean(values * values, axis=1, keepdims=True) + EPSILON)
    return (values * factor * gain_row).astype(jnp.bfloat16)


def whole(array):
    rank = len(array.shape)
    return pl.BlockSpec(array.shape, lambda *_: (0,) * rank)


def first_kernel(count, *refs):
    parts, gain_ref, w_ref, x_ref, o_ref = refs[:count], *refs[count:]

    @pl.when((pl.program_id(0) == 0) & (pl.program_id(1) == 0))
    def _():
        values = jnp.concatenate([p[...] for p in parts], axis=1).astype(jnp.float32)
        x_ref[...] = normed(values, gain_ref[...])

    o_ref[...] = dot(x_ref[...], w_ref[0], ((1,), (0,))).astype(o_ref.dtype)


def norm_and_pair(parts, gain, weight):
    rows = parts[0].shape[0]
    _, width, columns = weight.shape
    tile = tiles(columns, 256)
    count = columns // tile
    return pl.pallas_call(
        functools.partial(first_kernel, len(parts)),
        grid=(2, count),
        in_specs=[whole(p) for p in parts]
        + [whole(gain), pl.BlockSpec((1, width, tile), lambda i, n: (i, 0, n))],
        out_specs=[
            pl.BlockSpec((rows, width), lambda i, n: (0, 0)),
            pl.BlockSpec((rows, tile), lambda i, n: (0, i * count + n)),
        ],
        out_shape=[
            jax.ShapeDtypeStruct((rows, width), jnp.bfloat16),
            jax.ShapeDtypeStruct((rows, 2 * columns), jnp.bfloat16),
        ],
        compiler_params=PARAMS,
        cost_estimate=COST,
        name="norm_and_pair",
    )(*parts, gain, weight)


def product_kernel(x_ref, w_ref, o_ref):
    o_ref[...] = dot(x_ref[...], w_ref[...], ((1,), (0,))).astype(o_ref.dtype)


def product(inputs, weight):
    rows, width = inputs.shape
    columns = weight.shape[1]
    tile = tiles(columns, 512 if width > 2048 else 768)
    return pl.pallas_call(
        product_kernel,
        grid=(columns // tile,),
        in_specs=[whole(inputs), pl.BlockSpec((width, tile), lambda n: (0, n))],
        out_specs=pl.BlockSpec((rows, tile), lambda n: (0, n)),
        out_shape=jax.ShapeDtypeStruct((rows, columns), jnp.bfloat16),
        compiler_params=PARAMS,
        cost_estimate=COST,
        name="product",
    )(inputs, weight)


def window_kernel(group, info_ref, q_ref, kp_ref, ko_ref, vp_ref, vo_ref, o_ref):
    rows, width = ko_ref.shape
    head = pl.program_id(0)
    q = jnp.concatenate([q_ref[:, g * width : (g + 1) * width] for g in range(group)], axis=0)
    keys = jnp.concatenate([kp_ref[...], ko_ref[...]], axis=0)
    values = jnp.concatenate([vp_ref[...], vo_ref[...]], axis=0)
    s = dot(q, keys, ((1,), (1,)))
    row = lax.broadcasted_iota(jnp.int32, (rows, 2 * rows), 0)
    col = lax.broadcasted_iota(jnp.int32, (rows, 2 * rows), 1)
    offset = row + rows - col
    seen = (offset >= 0) & ((col >= rows) | (info_ref[0] > 0))
    masks = [seen & (offset < info_ref[1 + head * group + g]) for g in range(group)]
    s = jnp.concatenate(
        [jnp.where(masks[g], s[g * rows : (g + 1) * rows], MASKED) for g in range(group)], axis=0
    )
    weights = jnp.exp2((s - jnp.max(s, axis=1, keepdims=True)) * SCALE)
    total = jnp.sum(weights, axis=1, keepdims=True)
    acc = dot(weights.astype(jnp.bfloat16), values, ((1,), (0,))) / total
    for g in range(group):
        o_ref[:, g * width : (g + 1) * width] = acc[g * rows : (g + 1) * rows].astype(o_ref.dtype)


def window_attention(info, query, before, own, kv_heads):
    rows, columns = query.shape
    group = columns // (kv_heads * HEAD_WIDTH)
    queries = pl.BlockSpec((rows, group * HEAD_WIDTH), lambda h, _: (0, h))
    keys = pl.BlockSpec((rows, HEAD_WIDTH), lambda h, _: (0, h))
    values = pl.BlockSpec((rows, HEAD_WIDTH), lambda h, _: (0, kv_heads + h))
    return pl.pallas_call(
        functools.partial(window_kernel, group),
        grid_spec=pltpu.PrefetchScalarGridSpec(
            num_scalar_prefetch=1,
            grid=(kv_heads,),
            in_specs=[queries, keys, keys, values, values],
            out_specs=queries,
        ),
        out_shape=jax.ShapeDtypeStruct((rows, columns), jnp.bfloat16),
        compiler_params=PARAMS,
        cost_estimate=COST,
        name="window_attention",
    )(info, query, before, own, before, own)


def cache_kernel(count, chips, addends, ids_ref, *refs):
    parts, sums = refs[:count], refs[count : count + addends]
    gain_ref, w_ref, o_ref, mine_ref, others_ref, x_ref, t_ref = refs[count + addends :]
    shard = mine_ref.shape[0] // chips

    @pl.when((pl.program_id(0) == 0) & (pl.program_id(1) == 0))
    def _():
        values = jnp.concatenate([p[...] for p in parts], axis=1).astype(jnp.float32)
        values = values + added([ref[...] for ref in sums])
        x_ref[...] = normed(values, gain_ref[...])
        t_ref[...] = values.T

    o_ref[...] = dot(x_ref[...], w_ref[0], ((1,), (0,))).astype(o_ref.dtype)

    @pl.when((pl.program_id(0) == 1) & (pl.program_id(1) == pl.num_programs(1) - 1))
    def _():
        for j in range(chips):
            for k, ref in enumerate((mine_ref, others_ref)):
                at = pl.multiple_of(ids_ref[k * chips + j] * shard, shard)
                ref[j * shard : (j + 1) * shard, :] = t_ref[pl.ds(at, shard), :]


def cache_and_state(ids, parts, sums, gain, weight, chips):
    rows = parts[0].shape[0]
    _, width, columns = weight.shape
    tile = tiles(columns, 256)
    count = columns // tile
    held = width // CORES
    return pl.pallas_call(
        functools.partial(cache_kernel, len(parts), chips, len(sums)),
        grid_spec=pltpu.PrefetchScalarGridSpec(
            num_scalar_prefetch=1,
            grid=(2, count),
            in_specs=[whole(p) for p in parts]
            + [whole(p) for p in sums]
            + [whole(gain), pl.BlockSpec((1, width, tile), lambda i, n, _: (i, 0, n))],
            out_specs=[
                pl.BlockSpec((rows, tile), lambda i, n, _: (0, i * count + n)),
                pl.BlockSpec((held, rows), lambda i, n, _: (0, 0)),
                pl.BlockSpec((held, rows), lambda i, n, _: (0, 0)),
            ],
            scratch_shapes=[pltpu.VMEM((rows, width), jnp.bfloat16), pltpu.VMEM((width, rows), jnp.float32)],
        ),
        out_shape=[
            jax.ShapeDtypeStruct((rows, 2 * columns), jnp.bfloat16),
            jax.ShapeDtypeStruct((held, rows), jnp.float32),
            jax.ShapeDtypeStruct((held, rows), jnp.float32),
        ],
        compiler_params=PARAMS,
        cost_estimate=COST,
        name="cache_and_state",
    )(ids, *parts, *sums, gain, weight)


def fetch(refs, held, arrived):
    count = arrived.shape[0]
    shard = held.shape[0] // count
    copies = []
    for j in range(count):
        copies.append(pltpu.make_async_copy(refs[j].at[0], held.at[pl.ds(j * shard, shard)], arrived.at[j]))
        copies[-1].start()
    return copies


def added(sums):
    total = sums[0].astype(jnp.float32)
    for value in sums[1:]:
        total = total + value.astype(jnp.float32)
    return total


def query_kernel(states, addends, *refs):
    state_refs, sums = refs[:states], refs[states : states + addends]
    gain_ref, *refs = refs[states + addends :]
    *w_refs, new_ref, own_ref, twin_ref, square_ref, x_ref, held, arrived = refs
    tokens, features = x_ref.shape
    rows = tokens // CORES
    columns = own_ref.shape[1]
    tile = tiles(columns, 512)
    copies = fetch(w_refs, held, arrived)
    squares = jnp.zeros((tokens, 1), jnp.float32)
    part = tiles(features, 512)
    for at in range(0, features, part):
        span = slice(at, at + part)
        value = jnp.concatenate([ref[span, :] for ref in state_refs], axis=1)
        if sums:
            value = value + added([ref[span, :] for ref in sums])
        new_ref[span, :] = value
        turned = value.T
        squares = squares + jnp.sum(turned * turned, axis=1, keepdims=True)
        x_ref[:, span] = (turned * gain_ref[:, span]).astype(jnp.bfloat16)
    square_ref[...] = jnp.broadcast_to(squares, square_ref.shape)
    for copy in copies:
        copy.wait()
    for at in range(0, columns, tile):
        span = slice(at, at + tile)
        acc = dot(x_ref[...], held[:, span], ((1,), (0,)))
        own_ref[:, span] = acc[:rows]
        twin_ref[:, span] = acc[rows:].astype(twin_ref.dtype)


def query_project(states, sums, gain, pieces):
    _, shard, columns = pieces[0].shape
    count = len(pieces)
    features = states[0].shape[0]
    tokens = sum(s.shape[1] for s in states)
    rows = tokens // CORES
    return pl.pallas_call(
        functools.partial(query_kernel, len(states), len(sums)),
        grid_spec=pltpu.PrefetchScalarGridSpec(
            num_scalar_prefetch=0,
            grid=(1,),
            in_specs=[whole(v) for v in (*states, *sums, gain)] + [pl.BlockSpec(memory_space=pl.ANY)] * len(pieces),
            out_specs=[
                pl.BlockSpec((features, tokens), lambda n: (0, 0)),
                pl.BlockSpec((rows, columns), lambda n: (0, 0)),
                pl.BlockSpec((rows, columns), lambda n: (0, 0)),
                pl.BlockSpec((tokens, 128), lambda n: (0, 0)),
            ],
            scratch_shapes=[
                pltpu.VMEM((tokens, features), jnp.bfloat16),
                pltpu.VMEM((features, columns), jnp.bfloat16),
                pltpu.SemaphoreType.DMA((count,)),
            ],
        ),
        out_shape=[
            jax.ShapeDtypeStruct((features, tokens), jnp.float32),
            jax.ShapeDtypeStruct((rows, columns), jnp.float32),
            jax.ShapeDtypeStruct((rows, columns), jnp.bfloat16),
            jax.ShapeDtypeStruct((tokens, 128), jnp.float32),
        ],
        compiler_params=pltpu.CompilerParams(vmem_limit_bytes=MOST),
        cost_estimate=COST,
        name="query_project",
    )(*states, *sums, gain, *pieces)


def listed_kernel(group, held, width_all, count, seen_ref, qo_ref, qt_ref, so_ref, st_ref, *refs):
    k_refs, v_refs, o_ref = refs[:count], refs[count : 2 * count], refs[2 * count]
    rows = qo_ref.shape[0]
    width = HEAD_WIDTH
    per = 4 if count % 4 == 0 else 1
    factor = lax.rsqrt((so_ref[...] + st_ref[...]) / width_all + EPSILON)
    own_row = lax.broadcasted_iota(jnp.int32, (rows, rows), 0)
    own_col = lax.broadcasted_iota(jnp.int32, (rows, rows), 1)
    causal = jnp.concatenate([own_col <= own_row] * group, axis=0)
    for head in range(held):
        lanes = slice(head * width, (head + 1) * width)
        heads = [slice((head * group + g) * width, (head * group + g + 1) * width) for g in range(group)]
        q = jnp.concatenate(
            [((qo_ref[:, at] + qt_ref[:, at].astype(jnp.float32)) * factor).astype(jnp.bfloat16) for at in heads],
            axis=0,
        )
        parts = []
        for start in range(0, count, per):
            keys = jnp.concatenate([ref[:, lanes] for ref in k_refs[start : start + per]], axis=0)
            s = dot(q, keys, ((1,), (1,)))
            pieces = []
            for i in range(per):
                piece = s[:, i * rows : (i + 1) * rows]
                allowed = causal if start + i == 0 else seen_ref[start + i] > 0
                pieces.append(jnp.where(allowed, piece, MASKED))
            parts.append(jnp.concatenate(pieces, axis=1))
        largest = functools.reduce(jnp.maximum, [jnp.max(p, axis=1, keepdims=True) for p in parts])
        total = jnp.zeros_like(largest)
        acc = jnp.zeros((group * rows, width), jnp.float32)
        for n, p in enumerate(parts):
            weights = jnp.exp2((p - largest) * SCALE)
            total = total + jnp.sum(weights, axis=1, keepdims=True)
            values = jnp.concatenate([ref[:, lanes] for ref in v_refs[n * per : (n + 1) * per]], axis=0)
            acc = acc + dot(weights.astype(jnp.bfloat16), values, ((1,), (0,)))
        acc = acc / total
        for g, at in enumerate(heads):
            o_ref[:, at] = acc[g * rows : (g + 1) * rows].astype(o_ref.dtype)


def listed_attention(seen, own, brought, squares, twin_squares, blocks, kv_heads, width_all):
    rows, columns = own.shape
    group = columns // (kv_heads * HEAD_WIDTH)
    held = HEADS_AT_ONCE if kv_heads % HEADS_AT_ONCE == 0 else 1
    steps = kv_heads // held
    queries = pl.BlockSpec((rows, held * group * HEAD_WIDTH), lambda h, _: (0, h))
    sides = pl.BlockSpec((rows, 128), lambda h, _: (0, 0))
    return pl.pallas_call(
        functools.partial(listed_kernel, group, held, width_all, len(blocks)),
        grid_spec=pltpu.PrefetchScalarGridSpec(
            num_scalar_prefetch=1,
            grid=(steps,),
            in_specs=[queries, queries, sides, sides]
            + [pl.BlockSpec((rows, held * HEAD_WIDTH), lambda h, _: (0, h)) for _ in blocks]
            + [pl.BlockSpec((rows, held * HEAD_WIDTH), lambda h, _: (0, steps + h)) for _ in blocks],
            out_specs=queries,
        ),
        out_shape=jax.ShapeDtypeStruct((rows, columns), jnp.bfloat16),
        compiler_params=PARAMS,
        cost_estimate=COST,
        name="listed_attention",
    )(seen, own, brought, squares, twin_squares, *blocks, *blocks)


def output_kernel(own_ref, other_ref, *refs):
    *w_refs, o_ref, held, arrived = refs
    copies = fetch(w_refs, held, arrived)
    context = jnp.concatenate([own_ref[...], other_ref[...]], axis=0)
    shard = held.shape[0] // len(copies)
    for j in range(0, len(copies), AT_ONCE):
        for copy in copies[j : j + AT_ONCE]:
            copy.wait()
        at = slice(j * shard, min(j + AT_ONCE, len(copies)) * shard)
        o_ref[at, :] = dot(held[at, :], context, ((1,), (1,))).astype(o_ref.dtype)


def output_project(own, other, pieces):
    _, shard, columns = pieces[0].shape
    count = len(pieces)
    tokens = own.shape[0] + other.shape[0]
    return pl.pallas_call(
        output_kernel,
        grid_spec=pltpu.PrefetchScalarGridSpec(
            num_scalar_prefetch=0,
            grid=(1,),
            in_specs=[whole(own), whole(other)] + [pl.BlockSpec(memory_space=pl.ANY)] * len(pieces),
            out_specs=pl.BlockSpec((count * shard, tokens), lambda n: (0, 0)),
            scratch_shapes=[
                pltpu.VMEM((count * shard, columns), jnp.bfloat16),
                pltpu.SemaphoreType.DMA((count,)),
            ],
        ),
        out_shape=jax.ShapeDtypeStruct((count * shard, tokens), jnp.bfloat16),
        compiler_params=pltpu.CompilerParams(vmem_limit_bytes=MOST),
        cost_estimate=COST,
        name="output_project",
    )(own, other, *pieces)


def last_output_kernel(heads, share, places_ref, own_ref, other_ref, state_ref, *refs):
    w_refs, refs = refs[: -2 * heads - 2], refs[-2 * heads - 2 :]
    own_refs, twin_refs, held, arrived = refs[:heads], refs[heads : 2 * heads], refs[-2], refs[-1]
    copies = fetch(w_refs, held, arrived)
    context = jnp.concatenate([own_ref[...], other_ref[...]], axis=0)
    rows = own_ref.shape[0]
    shard = held.shape[0] // len(copies)
    if len(copies) > 1:
        for ref in (*own_refs, *twin_refs):
            ref[...] = jnp.zeros_like(ref)
    for copy in copies:
        copy.wait()
    terms = dot(held[...], context, ((1,), (1,))).astype(jnp.bfloat16)
    for j in range(len(copies)):
        at = slice(j * shard, (j + 1) * shard)
        for k in range(heads):
            value = state_ref[at, :] + terms[at].astype(jnp.float32) if k == 0 else terms[at]
            if len(copies) == 1:
                own_refs[k][...] = value[:, :rows]
                twin_refs[k][...] = value[:, rows:]
                continue
            place = places_ref[j]

            @pl.when(place // share == k)
            def _(k=k, value=value, place=place):
                to = pl.ds(pl.multiple_of((place - k * share) * shard, shard), shard)
                own_refs[k][to, :] = value[:, :rows]
                twin_refs[k][to, :] = value[:, rows:]


def last_output_project(places, own, other, state, pieces, heads, share):
    _, shard, columns = pieces[0].shape
    count = len(pieces)
    rows = own.shape[0]
    held = ((share if count > 1 else 1) * shard, rows)
    return pl.pallas_call(
        functools.partial(last_output_kernel, heads, share),
        grid_spec=pltpu.PrefetchScalarGridSpec(
            num_scalar_prefetch=1,
            grid=(1,),
            in_specs=[whole(own), whole(other), whole(state)] + [pl.BlockSpec(memory_space=pl.ANY)] * count,
            out_specs=[pl.BlockSpec(held, lambda n, *_: (0, 0))] * (2 * heads),
            scratch_shapes=[
                pltpu.VMEM((count * shard, columns), jnp.bfloat16),
                pltpu.SemaphoreType.DMA((count,)),
            ],
        ),
        out_shape=[
            jax.ShapeDtypeStruct(held, jnp.float32 if k == 0 else jnp.bfloat16) for _ in range(2) for k in range(heads)
        ],
        compiler_params=pltpu.CompilerParams(vmem_limit_bytes=MOST),
        cost_estimate=COST,
        name="last_output_project",
    )(places, own, other, state, *pieces)


def result_kernel(heads, shard, at_ref, *refs):
    own, twin, own_late, twin_late = (refs[k * heads : (k + 1) * heads] for k in range(4))
    o_ref, turned = refs[4 * heads :]
    count = own[0].shape[0] // shard
    for k, (sums, late) in enumerate(((own, own_late), (twin, twin_late))):
        for j in range(count):
            span = slice(j * shard, (j + 1) * shard)
            to = pl.ds(pl.multiple_of(at_ref[k * (count + 1) + j] * shard, shard), shard)
            turned[to, :] = added([ref[span, :] for ref in sums])
        place = at_ref[k * (count + 1) + count]

        @pl.when(place >= 0)
        def _(late=late, place=place):
            to = pl.ds(pl.multiple_of(jnp.maximum(place, 0) * shard, shard), shard)
            turned[to, :] = added([ref[...] for ref in late])

    o_ref[...] = turned[...].T


def arrange(at, parts, shard):
    features, rows = parts[0][0].shape
    return pl.pallas_call(
        functools.partial(result_kernel, len(parts[0]), shard),
        grid_spec=pltpu.PrefetchScalarGridSpec(
            num_scalar_prefetch=1,
            grid=(1,),
            in_specs=[whole(v) for part in parts for v in part],
            out_specs=pl.BlockSpec((rows, CORES * features), lambda n, _: (0, 0)),
            scratch_shapes=[pltpu.VMEM((CORES * features, rows), jnp.float32)],
        ),
        out_shape=jax.ShapeDtypeStruct((rows, CORES * features), jnp.float32),
        compiler_params=PARAMS,
        cost_estimate=COST,
        name="arrange",
    )(at, *[v for part in parts for v in part])


def body(
    tokens,
    norm_gains,
    window,
    self_query,
    self_key_value,
    self_output,
    shared_key_value,
    cross_query,
    cross_output,
    key_blocks,
):
    seq_count = lax.axis_size("seq")
    head_count = lax.axis_size("head")
    seq_rank = lax.axis_index("seq")
    head_rank = lax.axis_index("head")
    rows = tokens.shape[0]
    model_width = self_query.shape[0]
    kv_heads = self_key_value.shape[2] // HEAD_WIDTH
    sections, shard = cross_query.shape[:2]
    chips = seq_count // CORES

    order = list(range(0, chips, 2)) + list(range(1, chips, 2))[::-1]
    place = np.argsort(np.array(order))
    rightward, leftward = [], []
    for core in range(CORES):
        ranks = [chip * CORES + core for chip in order]
        rightward += [(ranks[i], ranks[(i + 1) % chips]) for i in range(chips)]
        leftward += [(ranks[i], ranks[i - 1]) for i in range(chips)]
    twins = [(rank, rank ^ 1) for rank in range(seq_count)]

    my_core = seq_rank % CORES
    my_place = jnp.take(jnp.asarray(place, jnp.int32), seq_rank // CORES)
    ring_chips = jnp.take(jnp.asarray(order, jnp.int32), (my_place + jnp.arange(chips)) % chips)
    own_shards = ring_chips * CORES + my_core
    twin_shards = ring_chips * CORES + (1 - my_core)

    def to_twin(value):
        return lax.ppermute(value, "seq", twins)

    def head_shift(value, k):
        return lax.ppermute(value, "head", [(i, (i + k) % head_count) for i in range(head_count)])

    def over_heads(value):
        return [value] + [head_shift(value, k) for k in range(1, head_count)]

    events, hops, found = {}, {}, {}

    def tied(value, name):
        needed = [hop(*at) for at in DONE_BEFORE.get(name, ())]
        if not needed or not jax.tree.leaves(value):
            return value
        return lax.optimization_barrier((value, needed))[0]

    def hop(chain, step):
        if (chain, step) in hops:
            return hops[chain, step]
        more_right = chain % 2 == 1
        right = chips // 2 if more_right else chips - 1 - chips // 2
        left = chips - 1 - right
        if step == 0:
            value = chains[chain]
            found[chain] = {0: value}
            values = [value, value]
        else:
            values = list(hop(chain, step - 1))
        after = START_AFTER.get((chain, step))
        if after is not None:
            after = events[after] if isinstance(after, str) else hop(*after)
            values, _ = lax.optimization_barrier((values, after))
        if step < right:
            values[0] = lax.ppermute(values[0], "seq", rightward)
            found[chain][-(step + 1) % chips] = values[0]
        if step < left:
            values[1] = lax.ppermute(values[1], "seq", leftward)
            found[chain][step + 1] = values[1]
        hops[chain, step] = tuple(values)
        return hops[chain, step]

    def pieces_of(chain):
        for step in range(chips // 2):
            hop(chain, step)
        return [found[chain][j] for j in range(chips)]

    chains = {}
    for s in range(sections):
        chains[2 * s] = cross_query[s][None]
        chains[2 * s + 1] = cross_output[s].T[None]

    held = over_heads(tokens)
    parts = []
    for j in range(head_count):
        part = held[0]
        for k in range(1, head_count):
            part = jnp.where((head_rank - j) % head_count == k, held[k], part)
        parts.append(part)

    parts = tied(parts, "f0")
    first, own_pair = norm_and_pair(parts, norm_gains[0:1], self_key_value)
    before = lax.ppermute(own_pair, "seq", [(i, i + 1) for i in range(seq_count - 1)])
    query = product(first, self_query)
    info = jnp.concatenate([seq_rank.reshape(1).astype(jnp.int32), window])
    query = tied(query, "f1")
    context = window_attention(info, query, before, own_pair, kv_heads)
    sums = over_heads(product(context, self_output))

    sums = tied(sums, "f2")
    ids = jnp.concatenate([own_shards, twin_shards])
    own_cache, mine, others = cache_and_state(ids, parts, sums, norm_gains[1:2], shared_key_value, chips)
    chains[CACHE] = own_cache
    events["cache"] = own_cache
    own_blocks = pieces_of(CACHE)
    blocks = own_blocks + [to_twin(block) for block in own_blocks]
    at_blocks = jnp.concatenate([own_shards, twin_shards])
    seen = jnp.any(key_blocks[:, 0, :, None] == at_blocks[None, None, :], axis=1).astype(jnp.int32)
    states, sums = [mine, to_twin(others)], []
    gains = jnp.take(norm_gains.reshape(-1, seq_count, shard), own_shards, axis=1).reshape(-1, chips * shard)

    for s in range(sections):
        sums = tied(sums, f"y{s}")
        states = tied(states, f"q{s}")
        query_pieces = pieces_of(2 * s)
        state, own, for_twin, squares = query_project(states, sums, gains[2 + s][None], query_pieces)
        events[f"q{s}"] = for_twin
        brought = to_twin(for_twin)
        twin_squares = to_twin(squares[rows:])
        brought = tied(brought, f"a{s}")
        own = listed_attention(
            seen[s], own, brought, squares[:rows], twin_squares, blocks, kv_heads, model_width
        )
        events[f"a{s}"] = own
        own = tied(own, f"t{s}")
        other = to_twin(own)
        other = tied(other, f"o{s}")
        output_pieces = pieces_of(2 * s + 1)
        if s < sections - 1:
            partial = output_project(own, other, output_pieces)
            events[f"o{s}"] = partial
            states, sums = [state], over_heads(partial)

    per_head = seq_count // head_count
    share = chips // head_count
    of_head = own_shards // per_head
    ranks = jnp.arange(chips)
    before_it = (of_head[None, :] == of_head[:, None]) & (ranks[None, :] < ranks[:, None])
    slots = jnp.sum(before_it, axis=1, dtype=jnp.int32)
    head_slots = (of_head - head_rank) % head_count * share + slots
    late = chips // 2
    early_ones = [j for j in range(chips) if j != late]
    state_pieces = state.reshape(chips, shard, CORES * rows)
    early_state = jnp.concatenate([state_pieces[:late], state_pieces[late + 1 :]]).reshape(-1, CORES * rows)

    def exchanged(parts):
        own_parts, twin_parts = list(parts[:head_count]), [to_twin(part) for part in parts[head_count:]]
        for k in range(1, head_count):
            own_parts[k] = head_shift(own_parts[k], k)
            twin_parts[k] = head_shift(twin_parts[k], k)
        return [own_parts, twin_parts]

    early_parts = last_output_project(
        jnp.take(head_slots, jnp.asarray(early_ones)),
        own,
        other,
        early_state,
        [output_pieces[j] for j in early_ones],
        head_count,
        share,
    )
    early_parts = exchanged(early_parts)
    late_parts = exchanged(
        last_output_project(
            head_slots[late : late + 1], own, other, state_pieces[late], [output_pieces[late]], head_count, share
        )
    )
    columns = jnp.sum(
        jnp.where((head_slots[None, :] == jnp.arange(share)[:, None]), own_shards[None, :], 0), axis=1, dtype=jnp.int32
    )
    columns = columns - head_rank * per_head
    late_column = jnp.where(head_slots[late] < share, own_shards[late] - head_rank * per_head, -1)
    flip = 1 - 2 * my_core
    places = [columns, late_column[None], columns + flip, jnp.where(late_column >= 0, late_column + flip, -1)[None]]
    return arrange(jnp.concatenate(places).astype(jnp.int32), early_parts + late_parts, shard)


CACHE = -2
START_AFTER = {(1, 0): (0, 0), (2, 0): (1, 1), (3, 0): (2, 1), (4, 0): (3, 1), (5, 0): (4, 1)}
DONE_BEFORE = {"f0": [(0, 0)], "f1": [(0, 1)], "f2": [(1, 0)]}
HEADS_AT_ONCE = 4
AT_ONCE = 8


def solution(mesh):
    placed = (
        P("seq", "head"),
        P(),
        P("head"),
        P(None, "head"),
        P(None, None, "head"),
        P("head", None),
        P(None, None, "head"),
        P(None, "seq", "head"),
        P(None, "head", "seq"),
        P(None, "seq", None),
    )
    return jax.shard_map(body, mesh=mesh, in_specs=placed, out_specs=P("seq", "head"), check_vma=False)
```
